32 devices in a mesh: row: 4 (over y, x), col: 8 (over z, core).
Axes of the slice: x: 2, y: 2, z: 4, core: 2. Of those that a mesh axis runs over, the one named last changes fastest.
Arguments:
- sensitivity: bfloat16 [32, 4, 2, 256, 128], P(('row', 'col')), may hold values from -0.3984375 to 0.3984375
- tile_ids: int32 [32, 4, 2], P(('row', 'col')), may hold values from 0 to 31, as said below
- counts: int32 [32, 4], P(('row', 'col')), may hold values from 0 to 2, as said below
- weight_class: int32 [32, 256], P(('row', 'col')), may hold values from 0 to 3
Outputs:
- normal_matrix: float32 [16384, 16384], P('row', 'col')
The draws below stay inside these ranges and needn't reach their ends.
Inputs may be any that keep to these rules, and one draw needn't show every extreme that they name: `tile_ids`: within one station block and one row owner the 2 slots name distinct tiles. `counts`: slots at or beyond the count are padding; in every draw some station block uses all 2 slots of every row owner.
All inputs are finite; a program needn't handle non-finite values.
Results may differ from the reference program's by a relative error of at most 0.0003.
Values may be sent and summed in bfloat16 or wider, within the bound.
No kernel may reach another device: no remote copies, remote signals or barrier semaphores. Data moves between devices by JAX's collectives and lax.ppermute only.
A program may use at most 128 MiB of HBM per device.

```python
import jax
import jax.numpy as jnp
from jax import lax

TILE = 128
TILES = 128
CAP = 2
ROWS = 256
BLOCKS = 32
N_ROW = 4


def draw_tile_ids(key, part):
    per_row = TILES // N_ROW
    scores = jax.random.randint(key, (BLOCKS, N_ROW, per_row), 0, 1 << 20) * per_row
    scores = scores + jnp.arange(per_row, dtype=jnp.int32)
    order = jnp.argsort(scores, axis=-1, stable=True)
    return order[..., :CAP].astype(jnp.int32)


def draw_counts(key, part):
    first, second = jax.random.split(jax.random.fold_in(key, 7))
    counts = jax.random.randint(first, (BLOCKS, N_ROW), 0, CAP + 1)
    chosen = jax.random.randint(second, (), 0, BLOCKS)
    full = jnp.arange(BLOCKS, dtype=jnp.int32)[:, None] == chosen
    return jnp.where(full, CAP, counts).astype(jnp.int32)


def with_ends(drawn, key, least, top_value):
    spot = [jax.random.randint(jax.random.fold_in(key, axis), (), 0, length) for axis, length in enumerate(drawn.shape)]
    widest = drawn.shape.index(max(drawn.shape))
    neighbour = spot[:widest] + [(spot[widest] + 1) % drawn.shape[widest]] + spot[widest + 1:]
    return drawn.at[tuple(spot)].set(least).at[tuple(neighbour)].set(top_value)


def shard_levels(stream_key, dims, cuts, smallest, largest):
    level = 1.0
    for axis_at, parts in cuts:
        steps = jax.random.uniform(jax.random.fold_in(jax.random.fold_in(stream_key, 6), axis_at), (parts,), jnp.float32, smallest / len(cuts), largest / len(cuts))
        level = level * jnp.repeat(jnp.exp(steps), dims[axis_at] // parts).reshape((-1,) + (1,) * (len(dims) - 1 - axis_at))
    return level


def centred(own_key, dims, scale, most, cuts=(), kind=jnp.bfloat16):
    gain = shard_levels(own_key, dims, cuts, -0.22, 0.18) if cuts else 1.0
    result = jax.random.normal(own_key, dims, jnp.float32) * scale * gain
    return jnp.minimum(jnp.maximum(result, -most), most).astype(kind)


def setup_inputs(seed: int = 0) -> dict:
    arg_keys = jax.random.split(jax.random.key(seed), 5)
    sensitivity = centred(arg_keys[0], (BLOCKS, N_ROW, CAP, ROWS, TILE), 0.05, 0.3984375, ((0, 32),))
    tile_ids = draw_tile_ids(jax.random.fold_in(arg_keys[4], 71), 0)
    counts = draw_counts(jax.random.fold_in(arg_keys[4], 71), 0)
    weight_class = with_ends(jax.random.randint(arg_keys[3], (BLOCKS, ROWS), 0, 4), jax.random.fold_in(arg_keys[3], 1), 0, 3).astype(jnp.int32)
    return dict(sensitivity=sensitivity, tile_ids=tile_ids, counts=counts, weight_class=weight_class)


def station_scale(weight_class):
    levels = jnp.array([1.0, 0.5, 0.25, 0.125], jnp.float32)
    hits = weight_class[..., None] == jnp.arange(4, dtype=jnp.int32)
    return jnp.sum(jnp.where(hits, levels, jnp.float32(0.0)), axis=-1)


def reference(sensitivity, tile_ids, counts, weight_class):
    blocks, row_devices, slots, rows, width = sensitivity.shape
    per_row = TILES // row_devices
    live = jnp.arange(slots, dtype=jnp.int32)[None, None, :] < counts[:, :, None]
    factor = station_scale(weight_class)[:, None, None, :, None] * live[:, :, :, None, None].astype(jnp.float32)
    weighted = (sensitivity.astype(jnp.float32) * factor).astype(jnp.bfloat16)
    offsets = (jnp.arange(row_devices, dtype=jnp.int32) * per_row)[None, :, None]
    global_ids = (tile_ids + offsets).astype(jnp.int32).reshape(blocks, row_devices * slots)
    compact = jnp.transpose(weighted, (0, 3, 1, 2, 4)).reshape(blocks, rows, row_devices * slots * width)
    count_slots = row_devices * slots

    def add_block(index, normal):
        left = lax.dynamic_index_in_dim(compact, index, 0, keepdims=False)
        gram = jnp.dot(left.T, left, preferred_element_type=jnp.float32)
        gram = jnp.transpose(gram.reshape(count_slots, width, count_slots, width), (0, 2, 1, 3))
        ids = lax.dynamic_index_in_dim(global_ids, index, 0, keepdims=False)
        return normal.at[ids[:, None], :, ids[None, :], :].add(gram)

    normal = jnp.zeros((TILES, width, TILES, width), jnp.float32)
    normal = lax.fori_loop(0, blocks, add_block, normal)
    return normal.reshape(TILES * width, TILES * width)
```

```python
import functools

import jax
import jax.numpy as jnp
from jax import lax
from jax.experimental import pallas as pl
from jax.experimental.pallas import tpu as pltpu
from jax.sharding import PartitionSpec as P

TILES = 128
CORES = 2
META_ROWS = 8


def accumulate_kernel(
    n_row, n_chip, slots, per_row, per_col, width,
    place_ref, weight_ref, *refs,
):
    chunks = CORES * (n_chip + n_row)
    sources = refs[:chunks]
    out_ref = refs[chunks + 1]
    acc, left_buf, right_buf, gram_buf, touches, done, load_sem, store_sem = refs[chunks + 2 :]
    n_left = CORES * n_chip

    def load(index):
        target = left_buf.at[index] if index < n_left else right_buf.at[index - n_left]
        return pltpu.make_async_copy(sources[index], target, load_sem.at[index])

    for index in range(chunks):
        load(index).start()

    tiles = per_row * per_col
    stations = CORES * n_row * n_chip

    def clear(index, carry):
        touches[index] = 0
        done[index] = 0
        return carry

    lax.fori_loop(0, tiles + 1, clear, 0)

    def tile_of(station, i, j):
        left = place_ref[station, i]
        right = place_ref[station, slots + j]
        inside = jnp.logical_and(left >= 0, right >= 0)
        return jnp.where(inside, left * per_col + right, tiles)

    def count(station, carry):
        for i in range(slots):
            for j in range(slots):
                tile = tile_of(station, i, j)
                touches[tile] = touches[tile] + 1
        return carry

    lax.fori_loop(0, stations, count, 0)

    for index in range(chunks):
        load(index).wait()

    def store(tile):
        rows = pl.ds(pl.multiple_of(lax.div(tile, per_col) * width, width), width)
        columns = pl.ds(pl.multiple_of(lax.rem(tile, per_col) * width, width), width)
        return pltpu.make_async_copy(acc.at[tile], out_ref.at[rows, columns], store_sem)

    def station_step(station, stored):
        row = lax.rem(station, n_row)
        core_chip = lax.div(station, n_row)
        core = lax.div(core_chip, n_chip)
        chip = lax.rem(core_chip, n_chip)
        weights = weight_ref[pl.ds(station, 1), :]
        left = jnp.concatenate([left_buf[core_chip, row, i].T for i in range(slots)], axis=0)
        left = (left.astype(jnp.float32) * weights).astype(jnp.bfloat16)
        right = jnp.concatenate(
            [right_buf[core * n_row + row, chip, j] for j in range(slots)], axis=1
        )
        gram_buf[...] = jnp.dot(left, right, preferred_element_type=jnp.float32)
        for i in range(slots):
            for j in range(slots):
                tile = tile_of(station, i, j)
                seen = done[tile]
                gram = gram_buf[i * width : (i + 1) * width, j * width : (j + 1) * width]
                acc[tile] = jnp.where(seen == 0, gram, acc[tile] + gram)
                done[tile] = seen + 1
                last = jnp.logical_and(seen + 1 == touches[tile], tile < tiles)

                @pl.when(last)
                def _():
                    store(tile).start()

                stored = stored + last.astype(jnp.int32)
        return stored

    stored = lax.fori_loop(0, stations, station_step, 0)

    def drain(index, carry):
        store(0).wait()
        return carry

    lax.fori_loop(0, stored, drain, 0)


def accumulate(place, weights, left, right, zeros, per_row, per_col):
    n_chip = len(left) // CORES
    n_row = len(right) // CORES
    _, slots, rows, width = left[0].shape
    chunks = len(left) + len(right)
    tiles = per_row * per_col
    anywhere = pl.BlockSpec(memory_space=pl.ANY)
    return pl.pallas_call(
        functools.partial(accumulate_kernel, n_row, n_chip, slots, per_row, per_col, width),
        out_shape=jax.ShapeDtypeStruct(zeros.shape, zeros.dtype),
        in_specs=[
            pl.BlockSpec(memory_space=pltpu.SMEM),
            pl.BlockSpec(memory_space=pltpu.VMEM),
            *[anywhere] * (chunks + 1),
        ],
        out_specs=anywhere,
        scratch_shapes=[
            pltpu.VMEM((tiles + 1, width, width), jnp.float32),
            pltpu.VMEM((len(left), n_row, slots, rows, width), jnp.bfloat16),
            pltpu.VMEM((len(right), n_chip, slots, rows, width), jnp.bfloat16),
            pltpu.VMEM((slots * width, slots * width), jnp.float32),
            pltpu.SMEM((tiles + 1,), jnp.int32),
            pltpu.SMEM((tiles + 1,), jnp.int32),
            pltpu.SemaphoreType.DMA((chunks,)),
            pltpu.SemaphoreType.DMA,
        ],
        input_output_aliases={2 + chunks: 0},
        compiler_params=pltpu.CompilerParams(vmem_limit_bytes=56 * 1024 * 1024),
        cost_estimate=pl.CostEstimate(flops=10**9, bytes_accessed=16 * 2**20, transcendentals=0),
    )(place, weights, *left, *right, zeros)


def zero_kernel(out_ref, block, sem):
    block[...] = jnp.zeros_like(block)
    height = block.shape[0]
    copies = [
        pltpu.make_async_copy(block, out_ref.at[pl.ds(index * height, height)], sem.at[index])
        for index in range(out_ref.shape[0] // height)
    ]
    for copy in copies:
        copy.start()
    for copy in copies:
        copy.wait()


def zero_fill(height, width):
    step = 128
    return pl.pallas_call(
        zero_kernel,
        out_shape=jax.ShapeDtypeStruct((height, width), jnp.float32),
        out_specs=pl.BlockSpec(memory_space=pl.ANY),
        scratch_shapes=[
            pltpu.VMEM((step, width), jnp.float32),
            pltpu.SemaphoreType.DMA((height // step,)),
        ],
        cost_estimate=pl.CostEstimate(
            flops=0, bytes_accessed=height * width * 4, transcendentals=0
        ),
    )()


def local(sensitivity, tile_ids, counts, weight_class):
    n_row = lax.axis_size("row")
    n_col = lax.axis_size("col")
    n_chip = n_col // CORES
    r = lax.axis_index("row")
    c = lax.axis_index("col")
    z, core = c // CORES, c % CORES
    _, _, slots, rows, width = sensitivity.shape
    per_row = TILES // n_row
    per_col = TILES // n_col
    owned = sensitivity[0]

    def part(owner):
        return lax.dynamic_index_in_dim(owned, owner, 0, keepdims=False)

    def flip_row(value, j):
        return lax.ppermute(value, "row", [(i, i ^ j) for i in range(n_row)])

    def shift_chip(value, s):
        pairs = [(i, (i + CORES * s) % n_col) for i in range(n_col)]
        return lax.ppermute(value, "col", pairs)

    def flip_core(value):
        return lax.ppermute(value, "col", [(i, i ^ 1) for i in range(n_col)])

    live = jnp.arange(slots, dtype=jnp.int32) < counts[0, :, None]
    ids = jnp.where(live, tile_ids[0], -1).reshape(-1)
    ids = jnp.pad(ids, (0, width - n_row * slots)).reshape(1, width)
    own_meta = jnp.concatenate(
        [weight_class.reshape(rows // width, width), ids], axis=0
    )
    own_meta = jnp.pad(own_meta, ((0, META_ROWS - rows // width - 1), (0, 0)))
    meta = lax.all_gather(own_meta, ("row", "col"), axis=0, tiled=False)

    left = [jnp.stack([part(r)] + [flip_row(part(r ^ j), j) for j in range(1, n_row)])]
    right = jnp.stack(
        [part(z)] + [shift_chip(part((z + s) % n_chip), s) for s in range(1, n_chip)]
    )
    right = [right] + [flip_row(right, j) for j in range(1, n_row)]
    for s in range(1, n_chip):
        left.append(shift_chip(left[-1], 1))
    left = left + [flip_core(x) for x in left]
    right = right + [flip_core(x) for x in right]

    rel_core = jnp.arange(CORES, dtype=jnp.int32)[:, None, None]
    rel_chip = jnp.arange(n_chip, dtype=jnp.int32)[None, :, None]
    rel_row = jnp.arange(n_row, dtype=jnp.int32)[None, None, :]
    station = (
        (r ^ rel_row) * n_col + (z - rel_chip) % n_chip * CORES + (core ^ rel_core)
    ).reshape(-1)
    meta = meta[station]
    classes = meta[:, : rows // width].reshape(-1, rows)
    weights = jnp.where(
        classes == 0, 1.0, jnp.where(classes == 1, 0.25, jnp.where(classes == 2, 0.0625, 0.015625))
    ).astype(jnp.float32)
    ids = meta[:, rows // width, : n_row * slots].reshape(-1, n_row, slots)
    left_ids = lax.dynamic_index_in_dim(ids, r, 1, keepdims=False)
    right_ids = lax.dynamic_index_in_dim(ids, z, 1, keepdims=False) - core * per_col
    right_ids = jnp.where((right_ids >= 0) & (right_ids < per_col), right_ids, -1)
    place = jnp.concatenate([left_ids, right_ids], axis=1)

    zeros = zero_fill(per_row * width, per_col * width)
    return accumulate(place, weights, left, right, zeros, per_row, per_col)


def solution(mesh):
    in_specs = (
        P(("row", "col"), None, None, None, None),
        P(("row", "col"), None, None),
        P(("row", "col"), None),
        P(("row", "col"), None),
    )
    return jax.shard_map(
        local, mesh=mesh, in_specs=in_specs, out_specs=P("row", "col"), check_vma=False
    )
```

```python
import functools

import jax
import jax.numpy as jnp
from jax import lax
from jax.experimental import pallas as pl
from jax.experimental.pallas import tpu as pltpu
from jax.sharding import PartitionSpec as P

TILES = 128
CORES = 2
STREAMS = 2
META = 16
MIB = 1024 * 1024


def pack_kernel(n_row, n_chip, slots, sens_ref, class_ref, ids_ref, counts_ref, *outs):
    r = lax.axis_index("row")
    z = lax.div(lax.axis_index("col"), CORES)
    rows, width = sens_ref.shape[2:]
    classes = class_ref[...]
    scale = jnp.where(
        classes == 0, 1.0, jnp.where(classes == 1, 0.5, jnp.where(classes == 2, 0.25, 0.125))
    ).astype(jnp.float32)
    scale = jnp.broadcast_to(scale, (width, rows)).T

    def tile(owner, slot):
        return (sens_ref[owner, slot].astype(jnp.float32) * scale).astype(jnp.bfloat16)

    for j in range(n_row):
        owner = r ^ j
        for i in range(slots):
            outs[j][i] = tile(owner, i)

    lane = lax.broadcasted_iota(jnp.int32, (META, width), 1)
    meta = jnp.zeros((META, width), jnp.float32)
    for q in range(n_row):
        for i in range(slots):
            place = jnp.where(i < counts_ref[q], ids_ref[q, i], -1)
            meta = jnp.where(lane == q * slots + i, place.astype(jnp.float32), meta)
    meta = meta.astype(jnp.bfloat16)
    for s in range(n_chip):
        owner = lax.rem(z + s, n_chip)
        out = outs[n_row + s]
        for i in range(slots):
            out[i * rows : (i + 1) * rows] = tile(owner, i)
        out[slots * rows :] = meta


def pack(sensitivity, weight_class, tile_ids, counts, n_chip):
    n_row, slots, rows, width = sensitivity.shape
    vmem = pl.BlockSpec(memory_space=pltpu.VMEM)
    smem = pl.BlockSpec(memory_space=pltpu.SMEM)
    return pl.pallas_call(
        functools.partial(pack_kernel, n_row, n_chip, slots),
        out_shape=[jax.ShapeDtypeStruct((slots, rows, width), jnp.bfloat16)] * n_row
        + [jax.ShapeDtypeStruct((slots * rows + META, width), jnp.bfloat16)] * n_chip,
        in_specs=[vmem, vmem, smem, smem],
        out_specs=[vmem] * (n_row + n_chip),
    )(sensitivity, weight_class, tile_ids, counts)


def tile_of(place, station, r, z, core, i, j, slots, per_col, none):
    left = place[station, r * slots + i]
    right = place[station, z * slots + j] - core * per_col
    inside = (left >= 0) & (right >= 0) & (right < per_col)
    return jnp.where(inside, left * per_col + right, none)


def block_of(out_ref, tile, per_col, width):
    rows = pl.ds(pl.multiple_of(lax.div(tile, per_col) * width, width), width)
    columns = pl.ds(pl.multiple_of(lax.rem(tile, per_col) * width, width), width)
    return out_ref.at[rows, columns]


def gram_of(left, right, slots):
    a = jnp.concatenate([left(i).T for i in range(slots)], axis=0)
    b = jnp.concatenate([right(j) for j in range(slots)], axis=1)
    return jnp.dot(a, b, preferred_element_type=jnp.float32)


def main_kernel(n_row, n_chip, slots, per_row, per_col, *refs):
    last = n_chip - 1
    n_left = last * STREAMS * CORES
    n_right = n_row * CORES
    sources = refs[: n_left + n_right]
    out_ref, carry_ref, right_ref, slot_ref, tile_ref = refs[n_left + n_right + 1 :][:5]
    (acc, left_buf, right_buf, gram_buf, meta_buf, place, touches, done, owner,
     load_sem, meta_sem, right_sem, store_sem) = refs[n_left + n_right + 6 :]
    r = lax.axis_index("row")
    c = lax.axis_index("col")
    z, core = lax.div(c, CORES), lax.rem(c, CORES)
    rows, width = left_buf.shape[-2:]
    half = n_row // STREAMS
    tiles = per_row * per_col
    pairs = [(i, j) for i in range(slots) for j in range(slots)]

    def load(index):
        target = left_buf.at[index] if index < n_left else right_buf.at[index - n_left]
        return pltpu.make_async_copy(sources[index], target, load_sem.at[index])

    for index in [*range(n_left, n_left + n_right), *range(n_left)]:
        load(index).start()

    def clear(index, carry):
        touches[index] = 0
        done[index] = 0
        owner[index] = -1
        return carry

    lax.fori_loop(0, tiles + 1, clear, 0)

    for index in range(n_right):
        load(n_left + index).wait()
        for s in range(n_chip):
            meta = right_buf[index, s, slots * rows :].astype(jnp.float32)
            meta_buf[index * n_chip + s : index * n_chip + s + 1, :] = meta[:1].astype(jnp.int32)
    to_smem = pltpu.make_async_copy(meta_buf, place, meta_sem)
    to_smem.start()
    right_out = [
        pltpu.make_async_copy(
            right_buf.at[index, last, pl.ds(0, slots * rows)],
            right_ref.at[index],
            right_sem.at[index],
        )
        for index in range(n_right)
    ]
    for copy in right_out:
        copy.start()
    to_smem.wait()

    def find(station, i, j, none):
        return tile_of(place, station, r, z, core, i, j, slots, per_col, none)

    def number(index, used):
        for n, (i, j) in enumerate(pairs):
            tile = find(index * n_chip + last, i, j, tiles)
            held = owner[tile]
            fresh = (held < 0) & (tile < tiles)
            spot = jnp.where(tile == tiles, len(pairs) * n_right, jnp.where(fresh, used, held))
            slot_ref[index * len(pairs) + n] = 2 * spot + fresh.astype(jnp.int32)
            owner[tile] = jnp.where(tile == tiles, -1, spot)
            tile_ref[jnp.where(fresh, used, len(pairs) * n_right)] = tile
            used = used + fresh.astype(jnp.int32)
        return used

    used = lax.fori_loop(0, n_right, number, 0)
    tile_ref[len(pairs) * n_right] = used

    def station_of(step):
        s = lax.div(step, n_right)
        index = lax.rem(step, n_right)
        return s, index, index * n_chip + s

    def count(step, carry):
        _, _, station = station_of(step)
        for i, j in pairs:
            tile = find(station, i, j, tiles)
            touches[tile] = touches[tile] + 1
        return carry

    lax.fori_loop(0, last * n_right, count, 0)

    def store(tile):
        return pltpu.make_async_copy(
            acc.at[tile], block_of(out_ref, tile, per_col, width), store_sem
        )

    for index in range(n_left):
        load(index).wait()

    def add(step, stored):
        s, index, station = station_of(step)
        other, j_row = lax.div(index, n_row), lax.rem(index, n_row)
        stream, place_in = lax.div(j_row, half), lax.rem(j_row, half)
        source = (s * STREAMS + stream) * CORES + other
        gram_buf[...] = gram_of(
            lambda i: left_buf[source, place_in, i],
            lambda j: right_buf[index, s, j * rows : (j + 1) * rows],
            slots,
        )
        for i, j in pairs:
            tile = find(station, i, j, tiles)
            seen = done[tile]
            gram = gram_buf[i * width : (i + 1) * width, j * width : (j + 1) * width]
            acc[tile] = jnp.where(seen == 0, gram, acc[tile] + gram)
            done[tile] = seen + 1
            ready = (seen + 1 == touches[tile]) & (tile < tiles) & (owner[tile] < 0)

            @pl.when(ready)
            def _():
                store(tile).start()

            stored = stored + ready.astype(jnp.int32)
        return stored

    stored = lax.fori_loop(0, last * n_right, add, 0)

    def hand_on(spot, carry):
        tile = tile_ref[spot]
        carry_ref[spot] = jnp.where(done[tile] == 0, 0.0, acc[tile])
        return carry

    lax.fori_loop(0, used, hand_on, 0)

    def drain(index, carry):
        store(0).wait()
        return carry

    lax.fori_loop(0, stored, drain, 0)
    for copy in right_out:
        copy.wait()


def main_part(left, right, zeros, per_row, per_col):
    last, n_chip = len(left), len(left) + 1
    n_row = len(right) // CORES
    _, slots, rows, width = left[0][0][0].shape
    flat = [x for chip in left for stream in chip for x in stream]
    chunks = len(flat) + len(right)
    tiles = per_row * per_col
    pairs = slots * slots * len(right)
    stations = n_chip * len(right)
    anywhere = pl.BlockSpec(memory_space=pl.ANY)
    vmem = pl.BlockSpec(memory_space=pltpu.VMEM)
    smem = pl.BlockSpec(memory_space=pltpu.SMEM)
    return pl.pallas_call(
        functools.partial(main_kernel, n_row, n_chip, slots, per_row, per_col),
        out_shape=[
            jax.ShapeDtypeStruct(zeros.shape, zeros.dtype),
            jax.ShapeDtypeStruct((pairs + 1, width, width), jnp.float32),
            jax.ShapeDtypeStruct((len(right), slots * rows, width), jnp.bfloat16),
            jax.ShapeDtypeStruct((pairs,), jnp.int32),
            jax.ShapeDtypeStruct((pairs + 1,), jnp.int32),
        ],
        in_specs=[anywhere] * (chunks + 1),
        out_specs=[anywhere, vmem, anywhere, smem, smem],
        scratch_shapes=[
            pltpu.VMEM((tiles + 1, width, width), jnp.float32),
            pltpu.VMEM((len(flat), n_row // STREAMS, slots, rows, width), jnp.bfloat16),
            pltpu.VMEM((len(right), n_chip, slots * rows + META, width), jnp.bfloat16),
            pltpu.VMEM((slots * width, slots * width), jnp.float32),
            pltpu.VMEM((stations, width), jnp.int32),
            pltpu.SMEM((stations, width), jnp.int32),
            pltpu.SMEM((tiles + 1,), jnp.int32),
            pltpu.SMEM((tiles + 1,), jnp.int32),
            pltpu.SMEM((tiles + 1,), jnp.int32),
            pltpu.SemaphoreType.DMA((chunks,)),
            pltpu.SemaphoreType.DMA,
            pltpu.SemaphoreType.DMA((len(right),)),
            pltpu.SemaphoreType.DMA,
        ],
        input_output_aliases={chunks: 0},
        compiler_params=pltpu.CompilerParams(vmem_limit_bytes=52 * MIB),
        cost_estimate=pl.CostEstimate(flops=10**9, bytes_accessed=16 * MIB, transcendentals=0),
    )(*flat, *right, zeros)


def tail_kernel(n_row, slots, per_col, slot_ref, tile_ref, *refs):
    lefts = refs[: STREAMS * CORES]
    carry_ref, right_ref = refs[STREAMS * CORES : STREAMS * CORES + 2]
    out_ref, acc, gram_buf, store_sem = refs[STREAMS * CORES + 3 :]
    rows, width = lefts[0].shape[-2:]
    half = n_row // STREAMS
    pairs = [(i, j) for i in range(slots) for j in range(slots)]

    for other in range(CORES):
        for stream in range(STREAMS):
            left = lefts[stream * CORES + other]

            def add(place_in, carry, left=left, base=other * n_row + stream * half):
                index = base + place_in
                gram_buf[...] = gram_of(
                    lambda i: left[place_in, i],
                    lambda j: right_ref[index, j * rows : (j + 1) * rows],
                    slots,
                )
                for n, (i, j) in enumerate(pairs):
                    code = slot_ref[index * len(pairs) + n]
                    spot, fresh = lax.shift_right_logical(code, 1), code & 1
                    gram = gram_buf[i * width : (i + 1) * width, j * width : (j + 1) * width]
                    acc[spot] = jnp.where(fresh == 1, carry_ref[spot], acc[spot]) + gram
                return carry

            lax.fori_loop(0, half, add, 0)

    def store(spot):
        return pltpu.make_async_copy(
            acc.at[spot], block_of(out_ref, tile_ref[spot], per_col, width), store_sem
        )

    def start(spot, carry):
        store(spot).start()
        return carry

    def drain(spot, carry):
        store(spot).wait()
        return carry

    used = tile_ref[len(pairs) * CORES * n_row]
    lax.fori_loop(0, used, start, 0)
    lax.fori_loop(0, used, drain, 0)


def tail_part(left, carried, right, slot, tile, out, per_col):
    flat = [x for stream in left for x in stream]
    half, slots, _, width = flat[0].shape
    anywhere = pl.BlockSpec(memory_space=pl.ANY)
    vmem = pl.BlockSpec(memory_space=pltpu.VMEM)
    smem = pl.BlockSpec(memory_space=pltpu.SMEM)
    return pl.pallas_call(
        functools.partial(tail_kernel, half * STREAMS, slots, per_col),
        out_shape=jax.ShapeDtypeStruct(out.shape, out.dtype),
        in_specs=[smem, smem] + [vmem] * (len(flat) + 2) + [anywhere],
        out_specs=anywhere,
        scratch_shapes=[
            pltpu.VMEM(carried.shape, jnp.float32),
            pltpu.VMEM((slots * width, slots * width), jnp.float32),
            pltpu.SemaphoreType.DMA,
        ],
        input_output_aliases={len(flat) + 4: 0},
        compiler_params=pltpu.CompilerParams(vmem_limit_bytes=32 * MIB),
        cost_estimate=pl.CostEstimate(flops=3 * 10**8, bytes_accessed=8 * MIB, transcendentals=0),
    )(slot, tile, *flat, carried, right, out)


def zero_kernel(out_ref, block, sem):
    block[...] = jnp.zeros_like(block)
    height = block.shape[0]
    copies = [
        pltpu.make_async_copy(block, out_ref.at[pl.ds(index * height, height)], sem.at[index])
        for index in range(out_ref.shape[0] // height)
    ]
    for copy in copies:
        copy.start()
    for copy in copies:
        copy.wait()


def zero_fill(height, width):
    step = 128
    return pl.pallas_call(
        zero_kernel,
        out_shape=jax.ShapeDtypeStruct((height, width), jnp.float32),
        out_specs=pl.BlockSpec(memory_space=pl.ANY),
        scratch_shapes=[
            pltpu.VMEM((step, width), jnp.float32),
            pltpu.SemaphoreType.DMA((height // step,)),
        ],
        cost_estimate=pl.CostEstimate(
            flops=0, bytes_accessed=height * width * 4, transcendentals=0
        ),
    )()


def local(sensitivity, tile_ids, counts, weight_class):
    n_row = lax.axis_size("row")
    n_col = lax.axis_size("col")
    n_chip = n_col // CORES
    per_row = TILES // n_row
    per_col = TILES // n_col

    def flip_row(value, j):
        return lax.ppermute(value, "row", [(i, i ^ j) for i in range(n_row)])

    def shift_chip(value, s):
        pairs = [(i, (i + CORES * s) % n_col) for i in range(n_col)]
        return lax.ppermute(value, "col", pairs)

    def flip_core(value):
        return lax.ppermute(value, "col", [(i, i ^ 1) for i in range(n_col)])

    parts = pack(sensitivity[0], weight_class, tile_ids[0], counts[0], n_chip)
    to_row, to_chip = parts[:n_row], parts[n_row:]
    right = jnp.stack([to_chip[0]] + [shift_chip(to_chip[s], s) for s in range(1, n_chip)])
    plane = [to_row[0]] + [flip_row(to_row[j], j) for j in range(1, n_row)]
    half = n_row // STREAMS
    left = [[jnp.stack(plane[k * half : (k + 1) * half]) for k in range(STREAMS)]]
    for _ in range(1, n_chip):
        left.append([shift_chip(x, 1) for x in left[-1]])
    right = [right] + [flip_row(right, j) for j in range(1, n_row)]
    right = right + [flip_core(x) for x in right]
    left = [[[x, flip_core(x)] for x in chip] for chip in left]

    width = sensitivity.shape[-1]
    zeros = zero_fill(per_row * width, per_col * width)
    out, carried, right, slot, tile = main_part(left[:-1], right, zeros, per_row, per_col)
    return tail_part(left[-1], carried, right, slot, tile, out, per_col)


def solution(mesh):
    in_specs = (
        P(("row", "col"), None, None, None, None),
        P(("row", "col"), None, None),
        P(("row", "col"), None),
        P(("row", "col"), None),
    )
    return jax.shard_map(
        local, mesh=mesh, in_specs=in_specs, out_specs=P("row", "col"), check_vma=False
    )
```

```python
import functools

import jax
import jax.numpy as jnp
from jax import lax
from jax.experimental import pallas as pl
from jax.experimental.pallas import tpu as pltpu
from jax.sharding import PartitionSpec as P

TILES = 128
CORES = 2
STREAMS = 2
META = 16
FACTS = 3
MIB = 1024 * 1024


def scale_of(class_ref):
    classes = class_ref[...]
    return jnp.where(
        classes == 0, 1.0, jnp.where(classes == 1, 0.5, jnp.where(classes == 2, 0.25, 0.125))
    ).astype(jnp.float32)


def pack_right_kernel(n_chip, slots, sens_ref, class_ref, ids_ref, counts_ref, *refs):
    outs, meta_ref = refs[:n_chip], refs[n_chip]
    z = lax.div(lax.axis_index("col"), CORES)
    n_row, _, rows, width = sens_ref.shape
    scale = jnp.broadcast_to(scale_of(class_ref), (width, rows)).T
    meta_ref[...] = jnp.zeros_like(meta_ref)
    for q in range(n_row):
        meta_ref[q : q + 1, :slots] = ids_ref[q].astype(jnp.float32)
    meta_ref[n_row : n_row + 1, :n_row] = counts_ref[...].astype(jnp.float32)
    meta = meta_ref[...].astype(jnp.bfloat16)
    for s in range(n_chip):
        owner = lax.rem(z + s, n_chip)
        for i in range(slots):
            tile = sens_ref[owner, i].astype(jnp.float32) * scale
            outs[s][i * rows : (i + 1) * rows] = tile.astype(jnp.bfloat16)
        outs[s][slots * rows :] = meta


def pack_left_kernel(n_row, slots, sens_ref, class_ref, after_ref, *outs):
    r = lax.axis_index("row")
    width = sens_ref.shape[-1]
    scale = scale_of(class_ref)
    for j in range(n_row):
        for i in range(slots):
            tile = sens_ref[r ^ j, i].T.astype(jnp.float32) * scale
            outs[j][i * width : (i + 1) * width] = tile.astype(jnp.bfloat16)


def pack_right(sensitivity, weight_class, tile_ids, counts, n_chip):
    n_row, slots, rows, width = sensitivity.shape
    vmem = pl.BlockSpec(memory_space=pltpu.VMEM)
    return pl.pallas_call(
        functools.partial(pack_right_kernel, n_chip, slots),
        out_shape=[jax.ShapeDtypeStruct((slots * rows + META, width), jnp.bfloat16)] * n_chip,
        in_specs=[vmem] * 4,
        out_specs=[vmem] * n_chip,
        scratch_shapes=[pltpu.VMEM((META, width), jnp.float32)],
    )(sensitivity, weight_class, tile_ids, counts)


def pack_left(sensitivity, weight_class, after):
    n_row, slots, rows, width = sensitivity.shape
    vmem = pl.BlockSpec(memory_space=pltpu.VMEM)
    return pl.pallas_call(
        functools.partial(pack_left_kernel, n_row, slots),
        out_shape=[jax.ShapeDtypeStruct((slots * width, rows), jnp.bfloat16)] * n_row,
        in_specs=[vmem, vmem, pl.BlockSpec(memory_space=pl.ANY)],
        out_specs=[vmem] * n_row,
    )(sensitivity, weight_class, after)


def tile_of(place, station, r, z, core, i, j, per_col, none):
    left = place[FACTS * station, i]
    right = place[FACTS * station + 1, j] - core * per_col
    used = (i < place[FACTS * station + 2, r]) & (j < place[FACTS * station + 2, z])
    inside = used & (right >= 0) & (right < per_col)
    return jnp.where(inside, left * per_col + right, none)


def block_of(out_ref, tile, per_col, width):
    rows = pl.ds(pl.multiple_of(lax.div(tile, per_col) * width, width), width)
    columns = pl.ds(pl.multiple_of(lax.rem(tile, per_col) * width, width), width)
    return out_ref.at[rows, columns]


def main_kernel(n_row, n_chip, slots, per_row, per_col, *refs):
    last = n_chip - 1
    n_left = last * STREAMS * CORES
    n_right = n_row * CORES
    sources = refs[: n_left + n_right]
    out_ref, carry_ref, right_ref, slot_ref, tile_ref = refs[n_left + n_right + 2 :][:5]
    (acc, left_buf, right_buf, meta_buf, fact_buf, zero_buf, place, touches, owner, plan, has,
     load_sem, fact_sem, zero_sem, store_sem) = refs[n_left + n_right + 7 :]
    r = lax.axis_index("row")
    c = lax.axis_index("col")
    z, core = lax.div(c, CORES), lax.rem(c, CORES)
    width = acc.shape[-1]
    rows = left_buf.shape[-1]
    half = n_row // STREAMS
    tiles = per_row * per_col
    pairs = [(i, j) for i in range(slots) for j in range(slots)]

    def load(index):
        target = left_buf.at[index] if index < n_left else right_buf.at[index - n_left]
        return pltpu.make_async_copy(sources[index], target, load_sem.at[index])

    for index in [*range(n_left, n_left + n_right), *range(n_left)]:
        load(index).start()
    zero_buf[...] = jnp.zeros_like(zero_buf)
    clears = [
        pltpu.make_async_copy(zero_buf, touches, zero_sem.at[0]),
        pltpu.make_async_copy(zero_buf, owner, zero_sem.at[1]),
    ]
    for copy in clears:
        copy.start()

    for index in range(n_right):
        load(n_left + index).wait()
        for s in range(n_chip):
            station = index * n_chip + s
            meta_buf[station] = right_buf[index, s, slots * rows :].astype(jnp.float32)
            for n, fact in enumerate((r, z, n_row)):
                row = meta_buf[station, pl.ds(fact, 1), :].astype(jnp.int32)
                fact_buf[FACTS * station + n : FACTS * station + n + 1, :] = row
    to_smem = pltpu.make_async_copy(fact_buf, place, fact_sem)
    to_smem.start()
    for index in range(n_right):
        right_ref[index] = right_buf[index, last, : slots * rows]
    for copy in clears:
        copy.wait()
    to_smem.wait()

    def at(tile):
        return lax.div(tile, width), lax.rem(tile, width)

    def find(station, i, j):
        return tile_of(place, station, r, z, core, i, j, per_col, tiles)

    def count(index, carry):
        for s in range(last):
            for n, (i, j) in enumerate(pairs):
                tile = find(index * n_chip + s, i, j)
                before = touches[at(tile)]
                touches[at(tile)] = before + 1
                code = 2 * tile + (before == 0).astype(jnp.int32)
                plan[(index * last + s) * len(pairs) + n] = code
        return carry

    lax.fori_loop(0, n_right, count, 0)

    none = len(pairs) * n_right

    def number(index, used):
        for n, (i, j) in enumerate(pairs):
            tile = find(index * n_chip + last, i, j)
            held = owner[at(tile)]
            fresh = (held == 0) & (tile < tiles)
            spot = jnp.where(tile == tiles, none, jnp.where(fresh, used, held - 1))
            slot_ref[index * len(pairs) + n] = 2 * spot + fresh.astype(jnp.int32)
            owner[at(tile)] = jnp.where(tile == tiles, 0, spot + 1)
            tile_ref[jnp.where(fresh, used, none)] = tile
            has[spot] = touches[at(tile)]
            used = used + fresh.astype(jnp.int32)
        return used

    used = lax.fori_loop(0, n_right, number, 0)
    tile_ref[none] = used

    for index in range(n_left):
        load(index).wait()

    def store(tile):
        return pltpu.make_async_copy(
            acc.at[tile], block_of(out_ref, tile, per_col, width), store_sem
        )

    def add(index, stored):
        other, j_row = lax.div(index, n_row), lax.rem(index, n_row)
        stream, place_in = lax.div(j_row, half), lax.rem(j_row, half)
        for s in range(last):
            left = left_buf[(s * STREAMS + stream) * CORES + other, place_in]
            right = jnp.concatenate(
                [right_buf[index, s, j * rows : (j + 1) * rows] for j in range(slots)], axis=1
            )
            gram = jnp.dot(left, right, preferred_element_type=jnp.float32)
            for n, (i, j) in enumerate(pairs):
                code = plan[(index * last + s) * len(pairs) + n]
                tile, fresh = lax.shift_right_logical(code, 1), code & 1
                part = gram[i * width : (i + 1) * width, j * width : (j + 1) * width]
                acc[tile] = jnp.where(fresh == 1, part, acc[tile] + part)
        for n in range(last * len(pairs)):
            tile = lax.shift_right_logical(plan[index * last * len(pairs) + n], 1)
            rest = touches[at(tile)] - 1
            touches[at(tile)] = rest
            ready = (rest == 0) & (tile < tiles) & (owner[at(tile)] == 0)

            @pl.when(ready)
            def _():
                store(tile).start()

            stored = stored + ready.astype(jnp.int32)
        return stored

    stored = lax.fori_loop(0, n_right, add, 0)

    def hand_on(spot, carry):
        carry_ref[spot] = jnp.where(has[spot] == 0, 0.0, acc[tile_ref[spot]])
        return carry

    lax.fori_loop(0, used, hand_on, 0)

    def drain(index, carry):
        store(0).wait()
        return carry

    lax.fori_loop(0, stored, drain, 0)


def main_part(left, right, zeros, token, per_row, per_col):
    last, n_chip = len(left), len(left) + 1
    n_row = len(right) // CORES
    half, height, rows = left[0][0][0].shape
    width = right[0].shape[-1]
    slots = height // width
    flat = [x for chip in left for stream in chip for x in stream]
    chunks = len(flat) + len(right)
    tiles = per_row * per_col
    pairs = slots * slots * len(right)
    stations = n_chip * len(right)
    state = (tiles // width + 1, width)
    held = (
        (tiles + pairs + 2) * width * width * 4
        + len(flat) * half * height * rows * 2
        + len(right) * (n_chip + 1) * (slots * rows + META) * width * 2
        + stations * (META + 2 * FACTS) * width * 4
    )
    anywhere = pl.BlockSpec(memory_space=pl.ANY)
    vmem = pl.BlockSpec(memory_space=pltpu.VMEM)
    smem = pl.BlockSpec(memory_space=pltpu.SMEM)
    return pl.pallas_call(
        functools.partial(main_kernel, n_row, n_chip, slots, per_row, per_col),
        out_shape=[
            jax.ShapeDtypeStruct(zeros.shape, zeros.dtype),
            jax.ShapeDtypeStruct((pairs + 1, width, width), jnp.float32),
            jax.ShapeDtypeStruct((len(right), slots * rows, width), jnp.bfloat16),
            jax.ShapeDtypeStruct((pairs,), jnp.int32),
            jax.ShapeDtypeStruct((pairs + 1,), jnp.int32),
        ],
        in_specs=[anywhere] * (chunks + 2),
        out_specs=[anywhere, vmem, vmem, smem, smem],
        scratch_shapes=[
            pltpu.VMEM((tiles + 1, width, width), jnp.float32),
            pltpu.VMEM((len(flat), half, height, rows), jnp.bfloat16),
            pltpu.VMEM((len(right), n_chip, slots * rows + META, width), jnp.bfloat16),
            pltpu.VMEM((stations, META, width), jnp.float32),
            pltpu.VMEM((FACTS * stations, width), jnp.int32),
            pltpu.VMEM(state, jnp.int32),
            pltpu.SMEM((FACTS * stations, width), jnp.int32),
            pltpu.SMEM(state, jnp.int32),
            pltpu.SMEM(state, jnp.int32),
            pltpu.SMEM((pairs * last,), jnp.int32),
            pltpu.SMEM((pairs + 1,), jnp.int32),
            pltpu.SemaphoreType.DMA((chunks,)),
            pltpu.SemaphoreType.DMA,
            pltpu.SemaphoreType.DMA((2,)),
            pltpu.SemaphoreType.DMA,
        ],
        input_output_aliases={chunks: 0},
        compiler_params=pltpu.CompilerParams(vmem_limit_bytes=held + 3 * MIB),
        cost_estimate=pl.CostEstimate(flops=0, bytes_accessed=0, transcendentals=0),
    )(*flat, *right, zeros, token)


def tail_kernel(n_row, slots, per_col, slot_ref, tile_ref, *refs):
    lefts = refs[: STREAMS * CORES]
    carry_ref, right_ref = refs[STREAMS * CORES : STREAMS * CORES + 2]
    out_ref, acc, store_sem = refs[STREAMS * CORES + 3 :]
    rows, width = lefts[0].shape[-1], acc.shape[-1]
    half = n_row // STREAMS
    pairs = [(i, j) for i in range(slots) for j in range(slots)]

    for index in range(CORES * n_row):
        other, j_row = index // n_row, index % n_row
        left = lefts[j_row // half * CORES + other][j_row % half]
        right = jnp.concatenate(
            [right_ref[index, j * rows : (j + 1) * rows] for j in range(slots)], axis=1
        )
        gram = jnp.dot(left, right, preferred_element_type=jnp.float32)
        for n, (i, j) in enumerate(pairs):
            code = slot_ref[index * len(pairs) + n]
            spot, fresh = lax.shift_right_logical(code, 1), code & 1
            part = gram[i * width : (i + 1) * width, j * width : (j + 1) * width]
            acc[spot] = jnp.where(fresh == 1, carry_ref[spot], acc[spot]) + part

    def store(spot):
        return pltpu.make_async_copy(
            acc.at[spot], block_of(out_ref, tile_ref[spot], per_col, width), store_sem
        )

    def start(spot, carry):
        store(spot).start()
        return carry

    def drain(spot, carry):
        store(spot).wait()
        return carry

    used = tile_ref[len(pairs) * CORES * n_row]
    lax.fori_loop(0, used, start, 0)
    lax.fori_loop(0, used, drain, 0)


def tail_part(left, carried, right, slot, tile, out, per_col):
    flat = [x for stream in left for x in stream]
    half, height, _ = flat[0].shape
    width = carried.shape[-1]
    anywhere = pl.BlockSpec(memory_space=pl.ANY)
    vmem = pl.BlockSpec(memory_space=pltpu.VMEM)
    smem = pl.BlockSpec(memory_space=pltpu.SMEM)
    return pl.pallas_call(
        functools.partial(tail_kernel, half * STREAMS, height // width, per_col),
        out_shape=jax.ShapeDtypeStruct(out.shape, out.dtype),
        in_specs=[smem, smem] + [vmem] * (len(flat) + 2) + [anywhere],
        out_specs=anywhere,
        scratch_shapes=[
            pltpu.VMEM(carried.shape, jnp.float32),
            pltpu.SemaphoreType.DMA,
        ],
        input_output_aliases={len(flat) + 4: 0},
        compiler_params=pltpu.CompilerParams(vmem_limit_bytes=24 * MIB),
        cost_estimate=pl.CostEstimate(flops=3 * 10**8, bytes_accessed=8 * MIB, transcendentals=0),
    )(slot, tile, *flat, carried, right, out)


def zero_kernel(first, count, *refs):
    out_ref, token_ref, block, sem = refs[-4:]
    block[...] = jnp.zeros_like(block)
    token_ref[...] = jnp.zeros_like(token_ref)
    height = block.shape[0]
    copies = [
        pltpu.make_async_copy(
            block, out_ref.at[pl.ds((first + index) * height, height)], sem.at[index]
        )
        for index in range(count)
    ]
    for copy in copies:
        copy.start()
    for copy in copies:
        copy.wait()


def zero_fill(height, width, half, after, out=None):
    step = 128
    count = height // step // 2
    inputs = [after] if out is None else [after, out]
    anywhere = pl.BlockSpec(memory_space=pl.ANY)
    return pl.pallas_call(
        functools.partial(zero_kernel, half * count, count),
        out_shape=[
            jax.ShapeDtypeStruct((height, width), jnp.float32),
            jax.ShapeDtypeStruct((8, 128), jnp.float32),
        ],
        in_specs=[anywhere] * len(inputs),
        out_specs=[anywhere, pl.BlockSpec(memory_space=pltpu.VMEM)],
        scratch_shapes=[
            pltpu.VMEM((step, width), jnp.float32),
            pltpu.SemaphoreType.DMA((count,)),
        ],
        input_output_aliases={} if out is None else {1: 0},
        cost_estimate=pl.CostEstimate(flops=0, bytes_accessed=0, transcendentals=0),
    )(*inputs)


def local(sensitivity, tile_ids, counts, weight_class):
    n_row = lax.axis_size("row")
    n_col = lax.axis_size("col")
    n_chip = n_col // CORES
    width = sensitivity.shape[-1]
    per_row = TILES // n_row
    per_col = TILES // n_col
    height, breadth = per_row * width, per_col * width

    def flip_row(value, j):
        return lax.ppermute(value, "row", [(i, i ^ j) for i in range(n_row)])

    def shift_chip(value, s):
        pairs = [(i, (i + CORES * s) % n_col) for i in range(n_col)]
        return lax.ppermute(value, "col", pairs)

    def flip_core(value):
        return lax.ppermute(value, "col", [(i, i ^ 1) for i in range(n_col)])

    after = lax.optimization_barrier

    ids = jnp.transpose(tile_ids, (1, 0, 2))
    to_chip = pack_right(sensitivity[0], weight_class, ids, counts, n_chip)
    to_row = pack_left(sensitivity[0], weight_class, to_chip[0])
    from_chip = [to_chip[0]] + [shift_chip(to_chip[s], s) for s in range(1, n_chip)]
    plane = [to_row[0]] + [flip_row(to_row[j], j) for j in range(1, n_row)]
    zeros, token = zero_fill(height, breadth, 0, to_row[0])
    from_chip, plane, token = after((from_chip, plane, token))

    half = n_row // STREAMS
    ring = [[jnp.stack(plane[k * half : (k + 1) * half]) for k in range(STREAMS)]]
    right = [jnp.stack(from_chip)]
    right += [flip_row(right[0], j) for j in range(1, n_row)]
    zeros, token = zero_fill(height, breadth, 1, token, zeros)
    for s in range(1, n_chip):
        ring.append([shift_chip(x, 1) for x in ring[-1]])
        if s == 1:
            ring[1], token = after((ring[1], token))
    left = [[[x, flip_core(x)] for x in chip] for chip in ring[:-1]]
    swapped = [flip_core(right[0])]
    others, before = after((right[1:], ring[-2]))
    left[-1] = [[x, flip_core(x)] for x in before]
    right = [right[0], *others, swapped[0], *(flip_core(x) for x in others)]

    out, carried, right, slot, tile = main_part(left, right, zeros, token, per_row, per_col)
    final, slot = after((ring[-1], slot))
    final = [[x, flip_core(x)] for x in final]
    return tail_part(final, carried, right, slot, tile, out, per_col)


def solution(mesh):
    in_specs = (
        P(("row", "col"), None, None, None, None),
        P(("row", "col"), None, None),
        P(("row", "col"), None),
        P(("row", "col"), None),
    )
    return jax.shard_map(
        local, mesh=mesh, in_specs=in_specs, out_specs=P("row", "col"), check_vma=False
    )
```

```python
import functools

import jax
import jax.numpy as jnp
from jax import lax
from jax.experimental import pallas as pl
from jax.experimental.pallas import tpu as pltpu
from jax.sharding import PartitionSpec as P

TILES = 128
CORES = 2
META = 16
EXTRA = 48
MIB = 1024 * 1024


def scale_of(class_ref):
    classes = class_ref[...]
    return jnp.where(
        classes == 0, 1.0, jnp.where(classes == 1, 0.5, jnp.where(classes == 2, 0.25, 0.125))
    ).astype(jnp.float32)


def pack_kernel(n_row, n_chip, slots, sens_ref, class_ref, ids_ref, counts_ref, *refs):
    outs, meta_ref = refs[:-1], refs[-1]
    r = lax.axis_index("row")
    z = lax.div(lax.axis_index("col"), CORES)
    rows, width = sens_ref.shape[2:]
    scale = scale_of(class_ref)
    for j in range(n_row):
        for i in range(slots):
            tile = sens_ref[r ^ j, i].T.astype(jnp.float32) * scale
            outs[j][i * width : (i + 1) * width] = tile.astype(jnp.bfloat16)
    scale = jnp.broadcast_to(scale, (width, rows)).T
    meta_ref[...] = jnp.zeros_like(meta_ref)
    meta_ref[:slots, :n_row] = ids_ref[...].astype(jnp.float32)
    meta_ref[slots : slots + 1, :n_row] = counts_ref[...].astype(jnp.float32)
    meta = meta_ref[...].astype(jnp.bfloat16)
    for s in range(n_chip):
        owner = lax.rem(z + s, n_chip)
        out = outs[n_row + s]
        for i in range(slots):
            tile = sens_ref[owner, i].astype(jnp.float32) * scale
            out[i * rows : (i + 1) * rows] = tile.astype(jnp.bfloat16)
        out[slots * rows :] = meta


def pack(sensitivity, weight_class, ids, counts, n_chip):
    n_row, slots, rows, width = sensitivity.shape
    vmem = pl.BlockSpec(memory_space=pltpu.VMEM)
    return pl.pallas_call(
        functools.partial(pack_kernel, n_row, n_chip, slots),
        out_shape=[jax.ShapeDtypeStruct((slots * width, rows), jnp.bfloat16)] * n_row
        + [jax.ShapeDtypeStruct((slots * rows + META, width), jnp.bfloat16)] * n_chip,
        in_specs=[vmem] * 4,
        out_specs=[vmem] * (n_row + n_chip),
        scratch_shapes=[pltpu.VMEM((META, width), jnp.float32)],
        cost_estimate=pl.CostEstimate(flops=0, bytes_accessed=0, transcendentals=0),
    )(sensitivity, weight_class, ids, counts)


def tile_of(place, station, r, z, core, i, j, slots, per_col, none):
    base = (slots + 1) * station
    left = place[base + i, r]
    right = place[base + j, z] - core * per_col
    used = (i < place[base + slots, r]) & (j < place[base + slots, z])
    inside = used & (right >= 0) & (right < per_col)
    return jnp.where(inside, left * per_col + right, none)


def block_of(out_ref, tile, per_col, width):
    rows = pl.ds(pl.multiple_of(lax.div(tile, per_col) * width, width), width)
    columns = pl.ds(pl.multiple_of(lax.rem(tile, per_col) * width, width), width)
    return out_ref.at[rows, columns]


def main_kernel(n_row, n_chip, slots, per_row, per_col, pieces, *refs):
    last = n_chip // 2
    others = [s for s in range(n_chip) if s != last]
    n_left = len(others) * CORES
    n_right = n_row * CORES
    n_source = n_left + len(pieces)
    sources = refs[:n_source]
    out_ref, right_ref, slot_ref, tile_ref = refs[n_source + 1 :][:4]
    (acc, left_buf, right_buf, fact_buf, zero_buf, blank, place, touches, owner, plan,
     load_sem, fact_sem, zero_sem, blank_sem, store_sem) = refs[n_source + 5 :]
    r = lax.axis_index("row")
    c = lax.axis_index("col")
    z, core = lax.div(c, CORES), lax.rem(c, CORES)
    width = acc.shape[-1]
    rows = left_buf.shape[-1]
    tiles = per_row * per_col
    facts = slots + 1
    pairs = [(i, j) for i in range(slots) for j in range(slots)]

    def load(index):
        if index < n_left:
            target = left_buf.at[index]
            source = sources[index].at[pl.ds(0, target.shape[0])]
        else:
            which, first, number = pieces[index - n_left]
            target = right_buf.at[which, pl.ds(first, number)]
            source = sources[index]
        return pltpu.make_async_copy(source, target, load_sem.at[index])

    for index in [*range(n_left, n_source), *range(n_left)]:
        load(index).start()
    zero_buf[...] = jnp.zeros_like(zero_buf)
    clears = [
        pltpu.make_async_copy(zero_buf, touches, zero_sem.at[0]),
        pltpu.make_async_copy(zero_buf, owner, zero_sem.at[1]),
    ]
    for copy in clears:
        copy.start()
    blank[...] = jnp.zeros_like(blank)
    step = blank.shape[0]
    top = out_ref.shape[0] // 2
    blanks = [
        pltpu.make_async_copy(blank, out_ref.at[pl.ds(top + n * step, step)], blank_sem.at[n])
        for n in range(top // step)
    ]
    for copy in blanks:
        copy.start()

    for index, (which, first, number) in enumerate(pieces):
        load(n_left + index).wait()
        for s in range(first, first + number):
            base = (which * n_chip + s) * facts
            meta = right_buf[which, s, slots * rows :].astype(jnp.float32)
            fact_buf[base : base + facts, :] = meta[:facts].astype(jnp.int32)
    to_smem = pltpu.make_async_copy(fact_buf, place, fact_sem)
    to_smem.start()
    for index in range(n_right):
        right_ref[index] = right_buf[index, last, : slots * rows]
    for copy in clears:
        copy.wait()
    to_smem.wait()

    def at(tile):
        return lax.div(tile, width), lax.rem(tile, width)

    def find(station, i, j):
        return tile_of(place, station, r, z, core, i, j, slots, per_col, tiles)

    none = len(pairs) * n_right

    def number_step(index, used):
        for n, (i, j) in enumerate(pairs):
            tile = find(index * n_chip + last, i, j)
            held = owner[at(tile)]
            fresh = (held == 0) & (tile < tiles)
            spot = jnp.where(tile == tiles, none, jnp.where(fresh, used, held - 1))
            slot_ref[index * len(pairs) + n] = 2 * spot + fresh.astype(jnp.int32)
            owner[at(tile)] = jnp.where(tile == tiles, 0, spot + 1)
            tile_ref[jnp.where(fresh, used, none)] = tile
            used = used + fresh.astype(jnp.int32)
        return used

    used = lax.fori_loop(0, n_right, number_step, 0)
    tile_ref[none] = used

    def plan_step(index, stored):
        for m, s in enumerate(others):
            for n, (i, j) in enumerate(pairs):
                tile = find(index * n_chip + s, i, j)
                fresh = touches[at(tile)] == 0
                touches[at(tile)] = 1
                own = fresh & (tile < tiles)
                code = 4 * tile + 2 * own.astype(jnp.int32) + fresh.astype(jnp.int32)
                plan[(index * len(others) + m) * len(pairs) + n] = code
                stored = stored + own.astype(jnp.int32)
        return stored

    stored = lax.fori_loop(0, n_right, plan_step, 0)

    for index in range(n_left):
        load(index).wait()

    def add(index, carry):
        other, j_row = lax.div(index, n_row), lax.rem(index, n_row)
        for m, s in enumerate(others):
            left = left_buf[m * CORES + other, pl.ds(j_row * slots * width, slots * width)]
            right = jnp.concatenate(
                [right_buf[index, s, j * rows : (j + 1) * rows] for j in range(slots)], axis=1
            )
            gram = jnp.dot(left, right, preferred_element_type=jnp.float32)
            for n, (i, j) in enumerate(pairs):
                code = plan[(index * len(others) + m) * len(pairs) + n]
                tile, fresh = lax.shift_right_logical(code, 2), code & 1
                part = gram[i * width : (i + 1) * width, j * width : (j + 1) * width]
                acc[tile] = jnp.where(fresh == 1, part, acc[tile] + part)
        return carry

    lax.fori_loop(0, n_right, add, 0)

    for copy in blanks:
        copy.wait()

    def store(tile):
        return pltpu.make_async_copy(
            acc.at[tile], block_of(out_ref, tile, per_col, width), store_sem
        )

    def store_step(index, carry):
        for n in range(len(others) * len(pairs)):
            code = plan[index * len(others) * len(pairs) + n]

            @pl.when(code & 2 != 0)
            def _():
                store(lax.shift_right_logical(code, 2)).start()

        return carry

    lax.fori_loop(0, n_right, store_step, 0)

    def drain_store(index, carry):
        store(0).wait()
        return carry

    lax.fori_loop(0, stored, drain_store, 0)


def main_part(left, right, pieces, zeros, n_row, per_row, per_col):
    n_chip = len(left) + 1
    n_right = n_row * CORES
    rows = left[0][0].shape[1]
    width = right[0].shape[-1]
    slots = right[0].shape[1] // rows
    height = n_row * slots * width
    flat = [x for chip in left for x in chip]
    chunks = len(flat) + len(right)
    tiles = per_row * per_col
    pairs = slots * slots * n_right
    facts = (n_chip * n_right * (slots + 1), width)
    state = (tiles // width + 1, width)
    step = width
    held = (
        (tiles + 1) * width * width * 4
        + len(flat) * height * rows * 2
        + n_right * (n_chip + 1) * (slots * rows + META) * width * 2
        + facts[0] * width * 4
        + step * zeros.shape[1] * 4
    )
    anywhere = pl.BlockSpec(memory_space=pl.ANY)
    vmem = pl.BlockSpec(memory_space=pltpu.VMEM)
    smem = pl.BlockSpec(memory_space=pltpu.SMEM)
    return pl.pallas_call(
        functools.partial(main_kernel, n_row, n_chip, slots, per_row, per_col, pieces),
        out_shape=[
            jax.ShapeDtypeStruct(zeros.shape, zeros.dtype),
            jax.ShapeDtypeStruct((n_right, slots * rows, width), jnp.bfloat16),
            jax.ShapeDtypeStruct((pairs,), jnp.int32),
            jax.ShapeDtypeStruct((pairs + 1,), jnp.int32),
        ],
        in_specs=[anywhere] * (chunks + 1),
        out_specs=[anywhere, vmem, smem, smem],
        scratch_shapes=[
            pltpu.VMEM((tiles + 1, width, width), jnp.float32),
            pltpu.VMEM((len(flat), height, rows), jnp.bfloat16),
            pltpu.VMEM((n_right, n_chip, slots * rows + META, width), jnp.bfloat16),
            pltpu.VMEM(facts, jnp.int32),
            pltpu.VMEM(state, jnp.int32),
            pltpu.VMEM((step, zeros.shape[1]), jnp.float32),
            pltpu.SMEM(facts, jnp.int32),
            pltpu.SMEM(state, jnp.int32),
            pltpu.SMEM(state, jnp.int32),
            pltpu.SMEM((pairs * len(left),), jnp.int32),
            pltpu.SemaphoreType.DMA((chunks,)),
            pltpu.SemaphoreType.DMA,
            pltpu.SemaphoreType.DMA((2,)),
            pltpu.SemaphoreType.DMA((zeros.shape[0] // 2 // step,)),
            pltpu.SemaphoreType.DMA,
        ],
        input_output_aliases={chunks: 0},
        compiler_params=pltpu.CompilerParams(vmem_limit_bytes=held + 3 * MIB),
        cost_estimate=pl.CostEstimate(flops=0, bytes_accessed=0, transcendentals=0),
    )(*flat, *right, zeros)


def tail_kernel(n_row, slots, per_col, slot_ref, tile_ref, *refs):
    lefts, right_ref = refs[:CORES], refs[CORES]
    out_ref, held, acc, load_sem, store_sem = refs[CORES + 2 :]
    rows, width = lefts[0].shape[-1], acc.shape[-1]
    pairs = [(i, j) for i in range(slots) for j in range(slots)]
    used = tile_ref[len(pairs) * CORES * n_row]

    def load(spot):
        tile = block_of(out_ref, tile_ref[spot], per_col, width)
        return pltpu.make_async_copy(tile, held.at[spot], load_sem)

    def store(spot):
        tile = block_of(out_ref, tile_ref[spot], per_col, width)
        return pltpu.make_async_copy(acc.at[spot], tile, store_sem)

    def each(act):
        def step(spot, carry):
            act(spot)
            return carry

        lax.fori_loop(0, used, step, 0)

    def gram_of(index):
        first = index % n_row * slots * width
        left = lefts[index // n_row][first : first + slots * width]
        right = jnp.concatenate(
            [right_ref[index, j * rows : (j + 1) * rows] for j in range(slots)], axis=1
        )
        return jnp.dot(left, right, preferred_element_type=jnp.float32)

    each(lambda spot: load(spot).start())
    for index in range(CORES * n_row):
        gram = gram_of(index)
        for n, (i, j) in enumerate(pairs):
            code = slot_ref[index * len(pairs) + n]
            spot, fresh = lax.shift_right_logical(code, 1), code & 1
            part = gram[i * width : (i + 1) * width, j * width : (j + 1) * width]
            acc[spot] = jnp.where(fresh == 1, part, acc[spot] + part)
    each(lambda spot: load(spot).wait())

    def add_store(spot):
        acc[spot] = acc[spot] + held[spot]
        store(spot).start()

    each(add_store)
    each(lambda spot: store(spot).wait())


def tail_part(left, right, slot, tile, out, per_col):
    rows = left[0].shape[1]
    n_row = right.shape[0] // CORES
    slots, width = right.shape[1] // rows, right.shape[2]
    spots = (slot.shape[0] + 1, width, width)
    anywhere = pl.BlockSpec(memory_space=pl.ANY)
    vmem = pl.BlockSpec(memory_space=pltpu.VMEM)
    smem = pl.BlockSpec(memory_space=pltpu.SMEM)
    return pl.pallas_call(
        functools.partial(tail_kernel, n_row, slots, per_col),
        out_shape=jax.ShapeDtypeStruct(out.shape, out.dtype),
        in_specs=[smem, smem] + [vmem] * (len(left) + 1) + [anywhere],
        out_specs=anywhere,
        scratch_shapes=[
            pltpu.VMEM(spots, jnp.float32),
            pltpu.VMEM(spots, jnp.float32),
            pltpu.SemaphoreType.DMA,
            pltpu.SemaphoreType.DMA,
        ],
        input_output_aliases={len(left) + 3: 0},
        compiler_params=pltpu.CompilerParams(vmem_limit_bytes=24 * MIB),
        cost_estimate=pl.CostEstimate(flops=0, bytes_accessed=0, transcendentals=0),
    )(slot, tile, *left, right, out)


def zero_kernel(after_ref, out_ref, block, sem):
    block[...] = jnp.zeros_like(block)
    height = block.shape[0]
    copies = [
        pltpu.make_async_copy(block, out_ref.at[pl.ds(n * height, height)], sem.at[n])
        for n in range(out_ref.shape[0] // 2 // height)
    ]
    for copy in copies:
        copy.start()
    for copy in copies:
        copy.wait()


def zero_upper(height, width, after):
    step = 128
    anywhere = pl.BlockSpec(memory_space=pl.ANY)
    return pl.pallas_call(
        zero_kernel,
        out_shape=jax.ShapeDtypeStruct((height, width), jnp.float32),
        in_specs=[anywhere],
        out_specs=anywhere,
        scratch_shapes=[
            pltpu.VMEM((step, width), jnp.float32),
            pltpu.SemaphoreType.DMA((height // 2 // step,)),
        ],
        cost_estimate=pl.CostEstimate(
            flops=0, bytes_accessed=height * width * 2, transcendentals=0
        ),
    )(after)


def local(sensitivity, tile_ids, counts, weight_class):
    n_row = lax.axis_size("row")
    n_col = lax.axis_size("col")
    n_chip = n_col // CORES
    width = sensitivity.shape[-1]
    per_row = TILES // n_row
    per_col = TILES // n_col
    middle = n_chip // 2

    def flip_row(value, j):
        return lax.ppermute(value, "row", [(i, i ^ j) for i in range(n_row)])

    def shift_chip(value, s):
        pairs = [(i, (i + CORES * s) % n_col) for i in range(n_col)]
        return lax.ppermute(value, "col", pairs)

    def flip_core(value):
        return lax.ppermute(value, "col", [(i, i ^ 1) for i in range(n_col)])

    after = lax.optimization_barrier

    ids = jnp.transpose(tile_ids, (0, 2, 1))[0]
    parts = pack(sensitivity[0], weight_class, ids, counts, n_chip)
    to_row, to_chip = parts[:n_row], parts[n_row:]
    plane = [to_row[0]] + [flip_row(to_row[j], j) for j in range(1, n_row)]
    from_chip = [to_chip[0]] + [shift_chip(to_chip[s], s) for s in range(1, n_chip)]
    zeros = zero_upper(per_row * width, per_col * width, to_chip[0])
    plane, from_chip, zeros = after((plane, from_chip, zeros))
    rows = sensitivity.shape[-2]
    chip = jnp.stack(plane).reshape(-1, rows)
    near = {0: chip}
    for s in range(1, middle):
        near[s] = shift_chip(near[s - 1], 1)
        near[n_chip - s] = shift_chip(near[(n_chip - s + 1) % n_chip], -1)
    right = jnp.stack(from_chip)
    sides = [right] + [flip_row(right, j) for j in range(1, n_row)]
    far = shift_chip(jnp.pad(near[middle - 1], ((0, EXTRA), (0, 0))), 1)
    near = after(near)
    swapped = {s: flip_core(near[s]) for s in near}
    swapped, waiting = after((swapped, sides))
    other_sides = [flip_core(x) for x in waiting]
    left = [[near[s], swapped[s]] for s in sorted(near)]
    pieces = [(j, 0, n_chip) for j in range(n_row * CORES)]

    out, tail_right, slot, tile = main_part(
        left, sides + other_sides, pieces, zeros, n_row, per_row, per_col
    )
    far, slot = after((far, slot))
    return tail_part([far, flip_core(far)], tail_right, slot, tile, out, per_col)


def solution(mesh):
    in_specs = (
        P(("row", "col"), None, None, None, None),
        P(("row", "col"), None, None),
        P(("row", "col"), None),
        P(("row", "col"), None),
    )
    return jax.shard_map(
        local, mesh=mesh, in_specs=in_specs, out_specs=P("row", "col"), check_vma=False
    )
```

```python
import functools

import jax
import jax.numpy as jnp
from jax import lax
from jax.experimental import pallas as pl
from jax.experimental.pallas import tpu as pltpu
from jax.sharding import PartitionSpec as P

TILES = 128
CORES = 2
META = 16
MIB = 1024 * 1024


def scale_of(class_ref):
    classes = class_ref[...]
    return jnp.where(
        classes == 0, 1.0, jnp.where(classes == 1, 0.5, jnp.where(classes == 2, 0.25, 0.125))
    ).astype(jnp.float32)


def pack_kernel(n_row, n_chip, slots, sens_ref, class_ref, ids_ref, counts_ref, *refs):
    outs, meta_ref = refs[:-1], refs[-1]
    r = lax.axis_index("row")
    z = lax.div(lax.axis_index("col"), CORES)
    rows, width = sens_ref.shape[2:]
    scale = scale_of(class_ref)
    for j in range(n_row):
        for i in range(slots):
            tile = sens_ref[r ^ j, i].T.astype(jnp.float32) * scale
            outs[j][i * width : (i + 1) * width] = tile.astype(jnp.bfloat16)
    scale = jnp.broadcast_to(scale, (width, rows)).T
    meta_ref[...] = jnp.zeros_like(meta_ref)
    meta_ref[:slots, :n_row] = ids_ref[...].astype(jnp.float32)
    meta_ref[slots : slots + 1, :n_row] = counts_ref[...].astype(jnp.float32)
    meta = meta_ref[...].astype(jnp.bfloat16)
    for s in range(n_chip):
        owner = lax.rem(z + s, n_chip)
        out = outs[n_row + s]
        for i in range(slots):
            tile = sens_ref[owner, i].astype(jnp.float32) * scale
            out[i * rows : (i + 1) * rows] = tile.astype(jnp.bfloat16)
        out[slots * rows :] = meta


def pack(sensitivity, weight_class, ids, counts, n_chip):
    n_row, slots, rows, width = sensitivity.shape
    vmem = pl.BlockSpec(memory_space=pltpu.VMEM)
    return pl.pallas_call(
        functools.partial(pack_kernel, n_row, n_chip, slots),
        out_shape=[jax.ShapeDtypeStruct((slots * width, rows), jnp.bfloat16)] * n_row
        + [jax.ShapeDtypeStruct((slots * rows + META, width), jnp.bfloat16)] * n_chip,
        in_specs=[vmem] * 4,
        out_specs=[vmem] * (n_row + n_chip),
        scratch_shapes=[pltpu.VMEM((META, width), jnp.float32)],
        cost_estimate=pl.CostEstimate(flops=0, bytes_accessed=0, transcendentals=0),
    )(sensitivity, weight_class, ids, counts)


def plan_of(facts, r, z, core, n_chip, slots, per_col, none):
    _, stations, width = facts.shape
    lane = lax.broadcasted_iota(jnp.int32, (stations, width), 1)

    def pick(row, owner):
        return jnp.sum(jnp.where(lane == owner, facts[row], 0.0), axis=1, keepdims=True)

    used_left, used_right = pick(slots, r), pick(slots, z)
    lefts = [pick(i, r) for i in range(slots)]
    rights = [pick(j, z) - (core * per_col).astype(jnp.float32) for j in range(slots)]
    column = []
    for i in range(slots):
        for j in range(slots):
            met = (i < used_left) & (j < used_right) & (rights[j] >= 0) & (rights[j] < per_col)
            column.append(jnp.where(met, lefts[i] * per_col + rights[j], float(none)))
    count = len(column) * stations
    tile = jnp.broadcast_to(jnp.concatenate(column, axis=0), (count, count))
    other = tile.T

    def facts_of(axis):
        pair = lax.broadcasted_iota(jnp.int32, (count, count), axis)
        station = lax.rem(pair, stations)
        far = lax.rem(station, n_chip) == n_chip // 2
        order = jnp.where(far, lax.div(station, n_chip), station) * len(column)
        return far, (order + lax.div(pair, stations)).astype(jnp.float32)

    far_down, order_down = facts_of(0)
    far_across, order_across = facts_of(1)
    same = (tile == other) & (far_down == far_across)
    first = jnp.min(jnp.where(same, order_down, 1e6), axis=0, keepdims=True)
    fresh = (first == order_across[:1]).astype(jnp.float32)
    real = (other[:1] < none).astype(jnp.float32)
    place = jnp.where(far_across[:1], first, other[:1])
    code = 4.0 * place + 2.0 * fresh * real + fresh
    return code.astype(jnp.int32), other[:1].astype(jnp.int32)


def block_of(out_ref, tile, per_col, width):
    rows = pl.ds(pl.multiple_of(lax.div(tile, per_col) * width, width), width)
    columns = pl.ds(pl.multiple_of(lax.rem(tile, per_col) * width, width), width)
    return out_ref.at[rows, columns]


def main_kernel(n_row, n_chip, slots, per_row, per_col, pieces, *refs):
    last = n_chip // 2
    others = [s for s in range(n_chip) if s != last]
    n_left = len(others) * CORES
    n_right = n_row * CORES
    n_source = n_left + len(pieces)
    sources = refs[:n_source]
    out_ref, right_ref, plan = refs[n_source + 1 :][:3]
    (acc, left_buf, right_buf, fact_buf, code_buf, blank,
     load_sem, code_sem, blank_sem, store_sem) = refs[n_source + 4 :]
    r = lax.axis_index("row")
    c = lax.axis_index("col")
    z, core = lax.div(c, CORES), lax.rem(c, CORES)
    width = acc.shape[-1]
    rows = left_buf.shape[-1]
    tiles = per_row * per_col
    stations = n_right * n_chip
    pairs = [(i, j) for i in range(slots) for j in range(slots)]

    def load(index):
        if index < n_left:
            target = left_buf.at[index]
            source = sources[index]
            if len(source.shape) == 2:
                source = source.at[pl.ds(0, target.shape[0])]
        else:
            which, first, number = pieces[index - n_left]
            target = right_buf.at[which, pl.ds(first, number)]
            source = sources[index]
        return pltpu.make_async_copy(source, target, load_sem.at[index])

    for index in [*range(n_left, n_source), *range(n_left)]:
        load(index).start()
    blank[...] = jnp.zeros_like(blank)
    step = blank.shape[0]
    top = out_ref.shape[0] // 2
    blanks = [
        pltpu.make_async_copy(blank, out_ref.at[pl.ds(top + n * step, step)], blank_sem.at[n])
        for n in range(top // step)
    ]
    for copy in blanks:
        copy.start()

    for index, (which, first, number) in enumerate(pieces):
        load(n_left + index).wait()
        for s in range(first, first + number):
            station = which * n_chip + s
            meta = right_buf[which, s, slots * rows :].astype(jnp.float32)
            for i in range(slots + 1):
                fact_buf[i, station : station + 1, :] = meta[i : i + 1]
    code, tile_row = plan_of(fact_buf, r, z, core, n_chip, slots, per_col, tiles)
    code_buf[0:1, :] = code
    code_buf[1:2, :] = tile_row
    to_smem = pltpu.make_async_copy(code_buf, plan, code_sem)
    to_smem.start()
    for index in range(n_right):
        right_ref[index] = right_buf[index, last, : slots * rows]
    to_smem.wait()

    for index in range(n_left):
        load(index).wait()

    def add(index, carry):
        other, j_row = lax.div(index, n_row), lax.rem(index, n_row)
        for m, s in enumerate(others):
            left = left_buf[m * CORES + other, pl.ds(j_row * slots * width, slots * width)]
            right = jnp.concatenate(
                [right_buf[index, s, j * rows : (j + 1) * rows] for j in range(slots)], axis=1
            )
            gram = jnp.dot(left, right, preferred_element_type=jnp.float32)
            for n, (i, j) in enumerate(pairs):
                code = plan[0, n * stations + index * n_chip + s]
                tile, fresh = lax.shift_right_logical(code, 2), code & 1
                part = gram[i * width : (i + 1) * width, j * width : (j + 1) * width]
                acc[tile] = jnp.where(fresh == 1, part, acc[tile] + part)
        return carry

    lax.fori_loop(0, n_right, add, 0)

    for copy in blanks:
        copy.wait()

    def store(tile):
        return pltpu.make_async_copy(
            acc.at[tile], block_of(out_ref, tile, per_col, width), store_sem
        )

    def store_step(index, stored):
        for s in others:
            for n in range(len(pairs)):
                code = plan[0, n * stations + index * n_chip + s]

                @pl.when(code & 2 != 0)
                def _():
                    store(lax.shift_right_logical(code, 2)).start()

                stored = stored + (lax.shift_right_logical(code, 1) & 1)
        return stored

    stored = lax.fori_loop(0, n_right, store_step, 0)

    def drain_store(index, carry):
        store(0).wait()
        return carry

    lax.fori_loop(0, stored, drain_store, 0)


def main_part(left, right, pieces, zeros, n_row, per_row, per_col):
    n_chip = len(left) + 1
    n_right = n_row * CORES
    rows = left[0][0].shape[1]
    width = right[0].shape[-1]
    slots = right[0].shape[1] // rows
    height = n_row * slots * width
    flat = [x for chip in left for x in chip]
    chunks = len(flat) + len(right)
    tiles = per_row * per_col
    pairs = slots * slots * n_right
    facts = (slots + 1, n_chip * n_right, width)
    plan = (8, pairs * n_chip)
    step = width
    held = (
        (tiles + 1) * width * width * 4
        + len(flat) * height * rows * 2
        + n_right * (n_chip + 1) * (slots * rows + META) * width * 2
        + facts[0] * facts[1] * width * 4
        + 8 * plan[1] * plan[1] * 4
        + step * zeros.shape[1] * 4
    )
    anywhere = pl.BlockSpec(memory_space=pl.ANY)
    vmem = pl.BlockSpec(memory_space=pltpu.VMEM)
    smem = pl.BlockSpec(memory_space=pltpu.SMEM)
    return pl.pallas_call(
        functools.partial(main_kernel, n_row, n_chip, slots, per_row, per_col, pieces),
        out_shape=[
            jax.ShapeDtypeStruct(zeros.shape, zeros.dtype),
            jax.ShapeDtypeStruct((n_right, slots * rows, width), jnp.bfloat16),
            jax.ShapeDtypeStruct(plan, jnp.int32),
        ],
        in_specs=[anywhere] * (chunks + 1),
        out_specs=[anywhere, vmem, smem],
        scratch_shapes=[
            pltpu.VMEM((tiles + 1, width, width), jnp.float32),
            pltpu.VMEM((len(flat), height, rows), jnp.bfloat16),
            pltpu.VMEM((n_right, n_chip, slots * rows + META, width), jnp.bfloat16),
            pltpu.VMEM(facts, jnp.float32),
            pltpu.VMEM(plan, jnp.int32),
            pltpu.VMEM((step, zeros.shape[1]), jnp.float32),
            pltpu.SemaphoreType.DMA((chunks,)),
            pltpu.SemaphoreType.DMA,
            pltpu.SemaphoreType.DMA((zeros.shape[0] // 2 // step,)),
            pltpu.SemaphoreType.DMA,
        ],
        input_output_aliases={chunks: 0},
        compiler_params=pltpu.CompilerParams(vmem_limit_bytes=held + 3 * MIB),
        cost_estimate=pl.CostEstimate(flops=0, bytes_accessed=0, transcendentals=0),
    )(*flat, *right, zeros)


def tail_kernel(n_row, n_chip, slots, per_col, plan, *refs):
    lefts, right_ref = refs[:CORES], refs[CORES]
    out_ref, held, acc, load_sem, store_sem = refs[CORES + 2 :]
    rows, width = lefts[0].shape[-1], acc.shape[-1]
    stations = CORES * n_row * n_chip
    pairs = [(i, j) for i in range(slots) for j in range(slots)]

    def at(index, n):
        return n * stations + index * n_chip + n_chip // 2

    def block(column):
        return block_of(out_ref, plan[1, column], per_col, width)

    def each_tile(act):
        def step(index, number):
            for n in range(len(pairs)):
                code = plan[0, at(index, n)]

                @pl.when(code & 2 != 0)
                def _():
                    act(lax.shift_right_logical(code, 2), at(index, n))

                number = number + (lax.shift_right_logical(code, 1) & 1)
            return number

        return lax.fori_loop(0, CORES * n_row, step, 0)

    def load(spot, column):
        return pltpu.make_async_copy(block(column), held.at[spot], load_sem)

    def store(spot, column):
        return pltpu.make_async_copy(acc.at[spot], block(column), store_sem)

    def gram_of(index):
        first = index % n_row * slots * width
        left = lefts[index // n_row][first : first + slots * width]
        right = jnp.concatenate(
            [right_ref[index, j * rows : (j + 1) * rows] for j in range(slots)], axis=1
        )
        return jnp.dot(left, right, preferred_element_type=jnp.float32)

    number = each_tile(lambda spot, column: load(spot, column).start())
    for index in range(CORES * n_row):
        gram = gram_of(index)
        for n, (i, j) in enumerate(pairs):
            code = plan[0, at(index, n)]
            spot, fresh = lax.shift_right_logical(code, 2), code & 1
            part = gram[i * width : (i + 1) * width, j * width : (j + 1) * width]
            acc[spot] = jnp.where(fresh == 1, part, acc[spot] + part)

    def wait_load(index, carry):
        pltpu.make_async_copy(held.at[0], held.at[0], load_sem).wait()
        return carry

    def wait_store(index, carry):
        pltpu.make_async_copy(held.at[0], held.at[0], store_sem).wait()
        return carry

    lax.fori_loop(0, number, wait_load, 0)

    def add_store(spot, column):
        acc[spot] = acc[spot] + held[spot]
        store(spot, column).start()

    each_tile(add_store)
    lax.fori_loop(0, number, wait_store, 0)


def tail_part(left, right, plan, out, per_col):
    rows = left[0].shape[1]
    n_row = right.shape[0] // CORES
    slots, width = right.shape[1] // rows, right.shape[2]
    pairs = slots * slots * CORES * n_row
    anywhere = pl.BlockSpec(memory_space=pl.ANY)
    vmem = pl.BlockSpec(memory_space=pltpu.VMEM)
    smem = pl.BlockSpec(memory_space=pltpu.SMEM)
    return pl.pallas_call(
        functools.partial(tail_kernel, n_row, plan.shape[1] // pairs, slots, per_col),
        out_shape=jax.ShapeDtypeStruct(out.shape, out.dtype),
        in_specs=[smem] + [vmem] * (len(left) + 1) + [anywhere],
        out_specs=anywhere,
        scratch_shapes=[
            pltpu.VMEM((pairs, width, width), jnp.float32),
            pltpu.VMEM((pairs, width, width), jnp.float32),
            pltpu.SemaphoreType.DMA,
            pltpu.SemaphoreType.DMA,
        ],
        input_output_aliases={len(left) + 2: 0},
        compiler_params=pltpu.CompilerParams(vmem_limit_bytes=24 * MIB),
        cost_estimate=pl.CostEstimate(flops=0, bytes_accessed=0, transcendentals=0),
    )(plan, *left, right, out)


def zero_kernel(after_ref, out_ref, block, sem):
    block[...] = jnp.zeros_like(block)
    height = block.shape[0]
    copies = [
        pltpu.make_async_copy(block, out_ref.at[pl.ds(n * height, height)], sem.at[n])
        for n in range(out_ref.shape[0] // 2 // height)
    ]
    for copy in copies:
        copy.start()
    for copy in copies:
        copy.wait()


def zero_upper(height, width, after):
    step = 128
    anywhere = pl.BlockSpec(memory_space=pl.ANY)
    return pl.pallas_call(
        zero_kernel,
        out_shape=jax.ShapeDtypeStruct((height, width), jnp.float32),
        in_specs=[anywhere],
        out_specs=anywhere,
        scratch_shapes=[
            pltpu.VMEM((step, width), jnp.float32),
            pltpu.SemaphoreType.DMA((height // 2 // step,)),
        ],
        cost_estimate=pl.CostEstimate(
            flops=0, bytes_accessed=height * width * 2, transcendentals=0
        ),
    )(after)


def local(sensitivity, tile_ids, counts, weight_class):
    n_row = lax.axis_size("row")
    n_col = lax.axis_size("col")
    n_chip = n_col // CORES
    width = sensitivity.shape[-1]
    per_row = TILES // n_row
    per_col = TILES // n_col
    middle = n_chip // 2

    def flip_row(value, j):
        return lax.ppermute(value, "row", [(i, i ^ j) for i in range(n_row)])

    def shift_chip(value, s):
        pairs = [(i, (i + CORES * s) % n_col) for i in range(n_col)]
        return lax.ppermute(value, "col", pairs)

    def flip_core(value):
        return lax.ppermute(value, "col", [(i, i ^ 1) for i in range(n_col)])

    def pad(value, extra):
        return jnp.pad(value, ((0, extra), (0, 0)))

    after = lax.optimization_barrier

    ids = jnp.transpose(tile_ids, (0, 2, 1))[0]
    parts = pack(sensitivity[0], weight_class, ids, counts, n_chip)
    to_row, to_chip = parts[:n_row], parts[n_row:]
    plane = [to_row[0]] + [flip_row(to_row[j], j) for j in range(1, n_row)]
    from_chip = [to_chip[0]] + [shift_chip(to_chip[s], s) for s in range(1, n_chip)]
    zeros = zero_upper(per_row * width, per_col * width, to_chip[0])
    plane, from_chip, zeros = after((plane, from_chip, zeros))
    rows = sensitivity.shape[-2]
    chip = jnp.stack(plane).reshape(-1, rows)
    near = {0: chip}
    for s in range(1, middle):
        near[s] = shift_chip(near[s - 1], 1)
        near[n_chip - s] = shift_chip(pad(chip, 48) if s == 1 else near[n_chip - s + 1], -1)
    right = jnp.stack(from_chip)
    own = [flip_core(chip), flip_core(right)]
    *own, again = after((*own, right))
    sides = [right] + [flip_row(right if j == 1 else again, j) for j in range(1, n_row)]
    far = shift_chip(pad(near[middle - 1], 64), 1)
    early = [s for s in near if 0 < s < middle]
    swapped = {s: flip_core(near[s]) for s in early}
    swapped, late, waiting = after(
        (swapped, {s: near[s] for s in near if s > middle}, sides[1:])
    )
    swapped |= {s: flip_core(late[s]) for s in late}
    swapped[0] = own[0]
    other_sides = [own[1]] + [flip_core(x) for x in waiting]
    left = [[near[s], swapped[s]] for s in sorted(near)]
    pieces = [(j, 0, n_chip) for j in range(n_row * CORES)]

    out, tail_right, plan = main_part(
        left, sides + other_sides, pieces, zeros, n_row, per_row, per_col
    )
    far, plan = after((far, plan))
    return tail_part([far, flip_core(far)], tail_right, plan, out, per_col)


def solution(mesh):
    in_specs = (
        P(("row", "col"), None, None, None, None),
        P(("row", "col"), None, None),
        P(("row", "col"), None),
        P(("row", "col"), None),
    )
    return jax.shard_map(
        local, mesh=mesh, in_specs=in_specs, out_specs=P("row", "col"), check_vma=False
    )
```

```python
import functools

import jax
import jax.numpy as jnp
from jax import lax
from jax.experimental import pallas as pl
from jax.experimental.pallas import tpu as pltpu
from jax.sharding import PartitionSpec as P

TILES = 128
CORES = 2
META = 16
ZERO_EARLY = 6
MIB = 1024 * 1024


def scale_of(class_ref):
    classes = class_ref[...]
    return jnp.where(
        classes == 0, 1.0, jnp.where(classes == 1, 0.5, jnp.where(classes == 2, 0.25, 0.125))
    ).astype(jnp.float32)


def pack_kernel(n_row, n_chip, slots, sens_ref, class_ref, ids_ref, counts_ref, *refs):
    outs, meta_ref = refs[:-1], refs[-1]
    r = lax.axis_index("row")
    z = lax.div(lax.axis_index("col"), CORES)
    rows, width = sens_ref.shape[2:]
    scale = scale_of(class_ref)
    for j in range(n_row):
        for i in range(slots):
            tile = sens_ref[r ^ j, i].T.astype(jnp.float32) * scale
            outs[j][i * width : (i + 1) * width] = tile.astype(jnp.bfloat16)
    scale = jnp.broadcast_to(scale, (width, rows)).T
    meta_ref[...] = jnp.zeros_like(meta_ref)
    meta_ref[:slots, :n_row] = ids_ref[...].astype(jnp.float32)
    meta_ref[slots : slots + 1, :n_row] = counts_ref[...].astype(jnp.float32)
    meta = meta_ref[...].astype(jnp.bfloat16)
    for s in range(n_chip):
        owner = lax.rem(z + s, n_chip)
        out = outs[n_row + s]
        for i in range(slots):
            tile = sens_ref[owner, i].astype(jnp.float32) * scale
            out[i * rows : (i + 1) * rows] = tile.astype(jnp.bfloat16)
        out[slots * rows :] = meta


def pack(sensitivity, weight_class, ids, counts, n_chip):
    n_row, slots, rows, width = sensitivity.shape
    vmem = pl.BlockSpec(memory_space=pltpu.VMEM)
    return pl.pallas_call(
        functools.partial(pack_kernel, n_row, n_chip, slots),
        out_shape=[jax.ShapeDtypeStruct((slots * width, rows), jnp.bfloat16)] * n_row
        + [jax.ShapeDtypeStruct((slots * rows + META, width), jnp.bfloat16)] * n_chip,
        in_specs=[vmem] * 4,
        out_specs=[vmem] * (n_row + n_chip),
        scratch_shapes=[pltpu.VMEM((META, width), jnp.float32)],
        cost_estimate=pl.CostEstimate(flops=0, bytes_accessed=0, transcendentals=0),
    )(sensitivity, weight_class, ids, counts)


def plan_of(facts, r, z, core, n_row, n_chip, slots, per_col, none, by_tile):
    _, stations, width = facts.shape
    lane = lax.broadcasted_iota(jnp.int32, (stations, width), 1)

    def pick(row, owner):
        return jnp.sum(jnp.where(lane == owner, facts[row], 0.0), axis=1, keepdims=True)

    used_left, used_right = pick(slots, r), pick(slots, z)
    lefts = [pick(i, r) for i in range(slots)]
    rights = [pick(j, z) - (core * per_col).astype(jnp.float32) for j in range(slots)]
    column = []
    for i in range(slots):
        for j in range(slots):
            met = (i < used_left) & (j < used_right) & (rights[j] >= 0) & (rights[j] < per_col)
            column.append(jnp.where(met, lefts[i] * per_col + rights[j], float(none)))
    count = len(column) * stations
    tile = jnp.broadcast_to(jnp.concatenate(column, axis=0), (count, count))
    other = tile.T

    def part_of(axis):
        pair = lax.broadcasted_iota(jnp.int32, (count, count), axis)
        station = lax.rem(pair, stations)
        s = lax.rem(station, n_chip)
        number = station * len(column) + lax.div(pair, stations)
        return s == n_chip // 2, number.astype(jnp.float32)

    tail_down, number_down = part_of(0)
    tail_across, number_across = part_of(1)
    same = (tile == other) & (tail_down == tail_across)
    first = jnp.min(jnp.where(same, number_down, 1e6), axis=0, keepdims=True)
    fresh = (first == number_across[:1]).astype(jnp.float32)
    last = jnp.max(jnp.where(same, number_down, -1.0), axis=0, keepdims=True)
    final = (last == number_across[:1]).astype(jnp.float32)
    real = (other[:1] < none).astype(jnp.float32)
    place = other[:1] if by_tile else first
    code = 8.0 * place + 4.0 * final * real + 2.0 * fresh * real + fresh
    return code.astype(jnp.int32), other[:1].astype(jnp.int32)


def settle(plan, groups, stations, slots, acc, held, out_ref, per_col, load_sem, store_sem):
    width = acc.shape[-1]
    pairs = slots * slots

    def copy(place, column, back):
        block = block_of(out_ref, plan[1, column], per_col, width)
        if back:
            return pltpu.make_async_copy(acc.at[place], block, store_sem)
        return pltpu.make_async_copy(block, held.at[place], load_sem)

    def each(columns, flag, act):
        number = 0
        for column in columns:
            for n in range(pairs):
                code = plan[0, column + n * stations]
                hit = lax.shift_right_logical(code, flag) & 1

                @pl.when(hit == 1)
                def _():
                    act(lax.shift_right_logical(code, 3), column + n * stations)

                number = number + hit
        return number

    def wait(number, sem):
        def step(index, carry):
            pltpu.make_async_copy(acc.at[0], acc.at[0], sem).wait()
            return carry

        lax.fori_loop(0, number, step, 0)

    def add(column, left, right):
        gram = jnp.dot(left(), right(), preferred_element_type=jnp.float32)
        for n in range(pairs):
            code = plan[0, column + n * stations]
            place, fresh = lax.shift_right_logical(code, 3), code & 1
            i, j = divmod(n, slots)
            part = gram[i * width : (i + 1) * width, j * width : (j + 1) * width]
            acc[place] = jnp.where(fresh == 1, part, acc[place] + part)

    def walk(act):
        total = 0
        for steps, stations_of in groups:
            if steps == 1:
                total = total + act(stations_of(0))
            else:
                total = lax.fori_loop(
                    0, steps, lambda step, sofar: sofar + act(stations_of(step)), total
                )
        return total

    def columns_of(found):
        return [column for column, _, _ in found]

    def start_loads(found):
        return each(columns_of(found), 1, lambda place, at: copy(place, at, False).start())

    def add_all(found):
        for column, left, right in found:
            add(column, left, right)
        return 0

    def add_store(found):
        add_all(found)
        return each(columns_of(found), 2, lambda place, at: copy(place, at, True).start())

    def finish(place, column):
        acc[place] = acc[place] + held[place]
        copy(place, column, True).start()

    if held is None:
        number = walk(add_store)
    else:
        number = walk(start_loads)
        walk(add_all)
        wait(number, load_sem)
        walk(lambda found: each(columns_of(found), 1, finish))
    wait(number, store_sem)


def parts_of(n_chip):
    far = n_chip // 2
    near = [s for s in range(n_chip) if s != far]
    return [near] * CORES, [[far]] * CORES


def block_of(out_ref, tile, per_col, width):
    rows = pl.ds(pl.multiple_of(lax.div(tile, per_col) * width, width), width)
    columns = pl.ds(pl.multiple_of(lax.rem(tile, per_col) * width, width), width)
    return out_ref.at[rows, columns]


def main_kernel(n_row, n_chip, slots, per_row, per_col, pieces, *refs):
    early, late = parts_of(n_chip)
    n_left = sum(map(len, early))
    n_source = n_left + len(pieces)
    sources = refs[:n_source]
    out_ref, right_ref, plan = refs[n_source + 1 :][:3]
    acc, left_buf, right_buf, fact_buf, code_buf = refs[n_source + 4 :][:5]
    load_sem, code_sem, store_sem = refs[n_source + 9 :]
    r = lax.axis_index("row")
    c = lax.axis_index("col")
    z, core = lax.div(c, CORES), lax.rem(c, CORES)
    rows, width = left_buf.shape[-1], acc.shape[-1]
    tiles = per_row * per_col
    stations = CORES * n_row * n_chip

    def load(index):
        if index < n_left:
            target = left_buf.at[index]
            source = sources[index].at[pl.ds(0, target.shape[0])]
        else:
            which, first, number = pieces[index - n_left]
            target = right_buf.at[which, pl.ds(first, number)]
            source = sources[index]
        return pltpu.make_async_copy(source, target, load_sem.at[index])

    for index in [*range(n_left, n_source), *range(n_left)]:
        load(index).start()
    for index, (which, first, number) in enumerate(pieces):
        load(n_left + index).wait()
        for s in range(first, first + number):
            station = which * n_chip + s
            meta = right_buf[which, s, slots * rows :].astype(jnp.float32)
            for i in range(slots + 1):
                fact_buf[i, station : station + 1, :] = meta[i : i + 1]
    code, tile_row = plan_of(
        fact_buf, r, z, core, n_row, n_chip, slots, per_col, tiles, acc.shape[0] > tiles
    )
    code_buf[0:1, :] = code
    code_buf[1:2, :] = tile_row
    to_smem = pltpu.make_async_copy(code_buf, plan, code_sem)
    to_smem.start()
    kept = 0
    for other in range(CORES):
        for j in range(n_row):
            for s in late[other]:
                right_ref[kept] = right_buf[other * n_row + j, s, : slots * rows]
                kept += 1
    for index in range(n_left):
        load(index).wait()
    to_smem.wait()

    def group(other):
        base = len(early[0]) * other

        def stations_of(j):
            index = other * n_row + j

            def station(m, s):
                def left():
                    return left_buf[base + m, pl.ds(j * slots * width, slots * width)]

                def right():
                    tiles = [right_buf[index, s, i * rows : (i + 1) * rows] for i in range(slots)]
                    return jnp.concatenate(tiles, axis=1)

                return index * n_chip + s, left, right

            return [station(m, s) for m, s in enumerate(early[other])]

        return n_row, stations_of

    groups = [group(other) for other in range(CORES)]
    settle(plan, groups, stations, slots, acc, None, out_ref, per_col, None, store_sem)


def main_part(left, right, pieces, out, n_row, per_row, per_col):
    n_chip = len(left[0]) + 1
    early, late = parts_of(n_chip)
    flat = [*left[0], *left[1]]
    rows, width = flat[0].shape[1], right[0].shape[2]
    slots = right[0].shape[1] // rows
    height = n_row * slots * width
    tiles = per_row * per_col
    stations = CORES * n_row * n_chip
    pairs = slots * slots * stations
    places = min(tiles + 1, pairs)
    plan = (8, pairs)
    sources = [*flat, *right]
    anywhere = pl.BlockSpec(memory_space=pl.ANY)
    held = (
        places * width * width * 4
        + len(flat) * height * rows * 2
        + (stations + n_row * sum(map(len, late))) * (slots * rows + META) * width * 2
        + (slots + 1) * stations * width * 4
        + 8 * pairs * pairs * 4
    )
    return pl.pallas_call(
        functools.partial(main_kernel, n_row, n_chip, slots, per_row, per_col, pieces),
        out_shape=[
            jax.ShapeDtypeStruct(out.shape, out.dtype),
            jax.ShapeDtypeStruct(
                (n_row * sum(map(len, late)), slots * rows, width), jnp.bfloat16
            ),
            jax.ShapeDtypeStruct(plan, jnp.int32),
        ],
        in_specs=[anywhere] * (len(sources) + 1),
        out_specs=[
            anywhere,
            pl.BlockSpec(memory_space=pltpu.VMEM),
            pl.BlockSpec(memory_space=pltpu.SMEM),
        ],
        scratch_shapes=[
            pltpu.VMEM((places, width, width), jnp.float32),
            pltpu.VMEM((len(flat), height, rows), jnp.bfloat16),
            pltpu.VMEM((CORES * n_row, n_chip, slots * rows + META, width), jnp.bfloat16),
            pltpu.VMEM((slots + 1, stations, width), jnp.float32),
            pltpu.VMEM(plan, jnp.int32),
            pltpu.SemaphoreType.DMA((len(sources),)),
            pltpu.SemaphoreType.DMA,
            pltpu.SemaphoreType.DMA,
        ],
        input_output_aliases={len(sources): 0},
        compiler_params=pltpu.CompilerParams(vmem_limit_bytes=held + 3 * MIB),
        cost_estimate=pl.CostEstimate(flops=0, bytes_accessed=0, transcendentals=0),
    )(*sources, out)


def tail_kernel(n_row, n_chip, slots, per_col, plan, *refs):
    _, late = parts_of(n_chip)
    n_left = sum(map(len, late))
    lefts, right_ref = refs[:n_left], refs[n_left]
    out_ref, acc, held, load_sem, store_sem = refs[n_left + 2 :]
    rows, width = lefts[0].shape[-1], acc.shape[-1]
    stations = CORES * n_row * n_chip

    found = []
    for other in range(CORES):
        for j in range(n_row):
            for m, s in enumerate(late[other]):
                source = lefts[len(late[0]) * other + m]

                def left(source=source, j=j):
                    return source[j * slots * width : (j + 1) * slots * width]

                def right(kept=len(found)):
                    tiles = [right_ref[kept, i * rows : (i + 1) * rows] for i in range(slots)]
                    return jnp.concatenate(tiles, axis=1)

                found.append(((other * n_row + j) * n_chip + s, left, right))
    groups = [(1, lambda step: found)]
    settle(plan, groups, stations, slots, acc, held, out_ref, per_col, load_sem, store_sem)


def tail_part(left, right, plan, out, n_row, per_row, per_col):
    flat = [*left[0], *left[1]]
    _, depth, width = right.shape
    slots = depth // flat[0].shape[1]
    stations = plan.shape[1] // slots**2
    n_chip = stations // (CORES * n_row)
    places = (min(per_row * per_col + 1, plan.shape[1]), width, width)
    anywhere = pl.BlockSpec(memory_space=pl.ANY)
    vmem = pl.BlockSpec(memory_space=pltpu.VMEM)
    smem = pl.BlockSpec(memory_space=pltpu.SMEM)
    held = 2 * places[0] * width * width * 4 + 2 * right.size * 2 + 2 * MIB * len(flat)
    return pl.pallas_call(
        functools.partial(tail_kernel, n_row, n_chip, slots, per_col),
        out_shape=jax.ShapeDtypeStruct(out.shape, out.dtype),
        in_specs=[smem] + [vmem] * (len(flat) + 1) + [anywhere],
        out_specs=anywhere,
        scratch_shapes=[
            pltpu.VMEM(places, jnp.float32),
            pltpu.VMEM(places, jnp.float32),
            pltpu.SemaphoreType.DMA,
            pltpu.SemaphoreType.DMA,
        ],
        input_output_aliases={len(flat) + 2: 0},
        compiler_params=pltpu.CompilerParams(vmem_limit_bytes=held + 4 * MIB),
        cost_estimate=pl.CostEstimate(flops=0, bytes_accessed=0, transcendentals=0),
    )(plan, *flat, right, out)


def zero_kernel(first, count, *refs):
    out_ref, block, sem = refs[-3:]
    block[...] = jnp.zeros_like(block)
    height = block.shape[0]
    copies = [
        pltpu.make_async_copy(block, out_ref.at[pl.ds((first + n) * height, height)], sem.at[n])
        for n in range(count)
    ]
    for copy in copies:
        copy.start()
    for copy in copies:
        copy.wait()


def zero_part(height, width, part, after, out=None):
    step = 128
    count = height // step
    early = count * ZERO_EARLY // 16
    first, number = ((0, early), (early, count - early))[part]
    anywhere = pl.BlockSpec(memory_space=pl.ANY)
    inputs = [after] if out is None else [after, out]
    return pl.pallas_call(
        functools.partial(zero_kernel, first, number),
        out_shape=jax.ShapeDtypeStruct((height, width), jnp.float32),
        in_specs=[anywhere] * len(inputs),
        out_specs=anywhere,
        scratch_shapes=[
            pltpu.VMEM((step, width), jnp.float32),
            pltpu.SemaphoreType.DMA((number,)),
        ],
        input_output_aliases={} if out is None else {1: 0},
        compiler_params=pltpu.CompilerParams(vmem_limit_bytes=4 * MIB),
        cost_estimate=pl.CostEstimate(
            flops=0, bytes_accessed=height * width * 2, transcendentals=0
        ),
    )(*inputs)


def local(sensitivity, tile_ids, counts, weight_class):
    n_row = lax.axis_size("row")
    n_col = lax.axis_size("col")
    n_chip = n_col // CORES
    width = sensitivity.shape[-1]
    per_row = TILES // n_row
    per_col = TILES // n_col
    middle = n_chip // 2

    def flip_row(value, j):
        return lax.ppermute(value, "row", [(i, i ^ j) for i in range(n_row)])

    def shift_chip(value, s):
        pairs = [(i, (i + CORES * s) % n_col) for i in range(n_col)]
        return lax.ppermute(value, "col", pairs)

    def flip_core(value):
        return lax.ppermute(value, "col", [(i, i ^ 1) for i in range(n_col)])

    def pad(value, extra):
        return jnp.pad(value, ((0, extra), (0, 0)))

    after = lax.optimization_barrier

    ids = jnp.transpose(tile_ids, (0, 2, 1))[0]
    parts = pack(sensitivity[0], weight_class, ids, counts, n_chip)
    to_row, to_chip = parts[:n_row], parts[n_row:]
    plane = [to_row[0]] + [flip_row(to_row[j], j) for j in range(1, n_row)]
    from_chip = [to_chip[0]] + [shift_chip(to_chip[s], s) for s in range(1, n_chip)]
    height, breadth = per_row * width, per_col * width
    zeros = zero_part(height, breadth, 0, to_chip[0])
    plane, from_chip, zeros = after((plane, from_chip, zeros))
    rows = sensitivity.shape[-2]
    chip = jnp.stack(plane).reshape(-1, rows)
    near = {0: chip}
    for s in range(1, middle):
        near[s] = shift_chip(near[s - 1], 1)
        near[n_chip - s] = shift_chip(pad(chip, 48) if s == 1 else near[n_chip - s + 1], -1)
    right = jnp.stack(from_chip)
    own = [flip_core(chip), flip_core(right)]
    *own, again, token = after((*own, right, to_chip[0]))
    sides = [right] + [flip_row(right if j == 1 else again, j) for j in range(1, n_row)]
    far = shift_chip(pad(near[middle - 1], 64), 1)
    swapped = {s: flip_core(near[s]) for s in range(1, middle)}
    zeros = zero_part(height, breadth, 1, token, zeros)
    swapped, late, waiting, zeros = after(
        (swapped, {s: near[s] for s in near if s > middle}, sides[1:], zeros)
    )
    swapped |= {s: flip_core(late[s]) for s in late} | {0: own[0]}
    sides += [own[1]] + [flip_core(x) for x in waiting]
    pieces = [(index, 0, n_chip) for index in range(CORES * n_row)]
    early = [[near[s] for s in sorted(near)], [swapped[s] for s in sorted(swapped)]]
    out, tail_right, plan = main_part(early, sides, pieces, zeros, n_row, per_row, per_col)
    far, plan = after((far, plan))
    return tail_part([[far], [flip_core(far)]], tail_right, plan, out, n_row, per_row, per_col)


def solution(mesh):
    in_specs = (
        P(("row", "col"), None, None, None, None),
        P(("row", "col"), None, None),
        P(("row", "col"), None),
        P(("row", "col"), None),
    )
    return jax.shard_map(
        local, mesh=mesh, in_specs=in_specs, out_specs=P("row", "col"), check_vma=False
    )
```

```python
import functools

import jax
import jax.numpy as jnp
from jax import lax
from jax.experimental import pallas as pl
from jax.experimental.pallas import tpu as pltpu
from jax.sharding import PartitionSpec as P

TILES = 128
CORES = 2
META = 16
ZERO_EARLY = 6
MIB = 1024 * 1024


def scale_of(class_ref):
    classes = class_ref[...]
    return jnp.where(
        classes == 0, 1.0, jnp.where(classes == 1, 0.5, jnp.where(classes == 2, 0.25, 0.125))
    ).astype(jnp.float32)


def pack_kernel(n_row, n_chip, slots, sens_ref, class_ref, ids_ref, counts_ref, *refs):
    outs, meta_ref = refs[:-1], refs[-1]
    r = lax.axis_index("row")
    z = lax.div(lax.axis_index("col"), CORES)
    rows, width = sens_ref.shape[2:]
    scale = scale_of(class_ref)
    for j in range(n_row):
        for i in range(slots):
            tile = sens_ref[r ^ j, i].T.astype(jnp.float32) * scale
            outs[j][i * width : (i + 1) * width] = tile.astype(jnp.bfloat16)
    scale = jnp.broadcast_to(scale, (width, rows)).T
    meta_ref[...] = jnp.zeros_like(meta_ref)
    meta_ref[:slots, :n_row] = ids_ref[...].astype(jnp.float32)
    meta_ref[slots : slots + 1, :n_row] = counts_ref[...].astype(jnp.float32)
    meta = meta_ref[...].astype(jnp.bfloat16)
    for s in range(n_chip):
        owner = lax.rem(z + s, n_chip)
        out = outs[n_row + s]
        for i in range(slots):
            tile = sens_ref[owner, i].astype(jnp.float32) * scale
            out[i * rows : (i + 1) * rows] = tile.astype(jnp.bfloat16)
        out[slots * rows :] = meta


def pack(sensitivity, weight_class, ids, counts, n_chip):
    n_row, slots, rows, width = sensitivity.shape
    vmem = pl.BlockSpec(memory_space=pltpu.VMEM)
    return pl.pallas_call(
        functools.partial(pack_kernel, n_row, n_chip, slots),
        out_shape=[jax.ShapeDtypeStruct((slots * width, rows), jnp.bfloat16)] * n_row
        + [jax.ShapeDtypeStruct((slots * rows + META, width), jnp.bfloat16)] * n_chip,
        in_specs=[vmem] * 4,
        out_specs=[vmem] * (n_row + n_chip),
        scratch_shapes=[pltpu.VMEM((META, width), jnp.float32)],
        cost_estimate=pl.CostEstimate(flops=0, bytes_accessed=0, transcendentals=0),
    )(sensitivity, weight_class, ids, counts)


def plan_of(facts, r, z, core, n_row, n_chip, slots, per_col, none, by_tile):
    _, stations, width = facts.shape
    lane = lax.broadcasted_iota(jnp.int32, (stations, width), 1)

    def pick(row, owner):
        return jnp.sum(jnp.where(lane == owner, facts[row], 0.0), axis=1, keepdims=True)

    used_left, used_right = pick(slots, r), pick(slots, z)
    lefts = [pick(i, r) for i in range(slots)]
    rights = [pick(j, z) - (core * per_col).astype(jnp.float32) for j in range(slots)]
    column = []
    for i in range(slots):
        for j in range(slots):
            met = (i < used_left) & (j < used_right) & (rights[j] >= 0) & (rights[j] < per_col)
            column.append(jnp.where(met, lefts[i] * per_col + rights[j], float(none)))
    count = len(column) * stations
    tile = jnp.broadcast_to(jnp.concatenate(column, axis=0), (count, count))
    other = tile.T

    def part_of(axis):
        pair = lax.broadcasted_iota(jnp.int32, (count, count), axis)
        station = lax.rem(pair, stations)
        s = lax.rem(station, n_chip)
        number = station * len(column) + lax.div(pair, stations)
        return s == n_chip // 2, number.astype(jnp.float32)

    tail_down, number_down = part_of(0)
    tail_across, number_across = part_of(1)
    same = (tile == other) & (tail_down == tail_across)
    first = jnp.min(jnp.where(same, number_down, 1e6), axis=0, keepdims=True)
    fresh = (first == number_across[:1]).astype(jnp.float32)
    last = jnp.max(jnp.where(same, number_down, -1.0), axis=0, keepdims=True)
    final = (last == number_across[:1]).astype(jnp.float32)
    real = (other[:1] < none).astype(jnp.float32)
    place = other[:1] if by_tile else first
    code = 8.0 * place + 4.0 * final * real + 2.0 * fresh * real + fresh
    return code.astype(jnp.int32), other[:1].astype(jnp.int32)


def settle(plan, groups, stations, slots, acc, held, out_ref, per_col, load_sem, store_sem):
    width = acc.shape[-1]
    pairs = slots * slots

    def copy(place, column, back):
        block = block_of(out_ref, plan[1, column], per_col, width)
        if back:
            return pltpu.make_async_copy(acc.at[place], block, store_sem)
        return pltpu.make_async_copy(block, held.at[place], load_sem)

    def each(columns, flag, act):
        number = 0
        for column in columns:
            for n in range(pairs):
                code = plan[0, column + n * stations]
                hit = lax.shift_right_logical(code, flag) & 1

                @pl.when(hit == 1)
                def _():
                    act(lax.shift_right_logical(code, 3), column + n * stations)

                number = number + hit
        return number

    def wait(number, sem):
        def step(index, carry):
            pltpu.make_async_copy(acc.at[0], acc.at[0], sem).wait()
            return carry

        lax.fori_loop(0, number, step, 0)

    def add(column, left, right):
        gram = jnp.dot(left(), right(), preferred_element_type=jnp.float32)
        for n in range(pairs):
            code = plan[0, column + n * stations]
            place, fresh = lax.shift_right_logical(code, 3), code & 1
            i, j = divmod(n, slots)
            part = gram[i * width : (i + 1) * width, j * width : (j + 1) * width]
            acc[place] = jnp.where(fresh == 1, part, acc[place] + part)

    def walk(act):
        total = 0
        for steps, stations_of in groups:
            if steps == 1:
                total = total + act(stations_of(0))
            else:
                total = lax.fori_loop(
                    0, steps, lambda step, sofar: sofar + act(stations_of(step)), total
                )
        return total

    def columns_of(found):
        return [column for column, _, _ in found]

    def start_loads(found):
        return each(columns_of(found), 1, lambda place, at: copy(place, at, False).start())

    def add_all(found):
        for column, left, right in found:
            add(column, left, right)
        return 0

    def add_store(found):
        add_all(found)
        return each(columns_of(found), 2, lambda place, at: copy(place, at, True).start())

    def finish(place, column):
        acc[place] = acc[place] + held[place]
        copy(place, column, True).start()

    if held is None:
        number = walk(add_store)
    else:
        number = walk(start_loads)
        walk(add_all)
        wait(number, load_sem)
        walk(lambda found: each(columns_of(found), 1, finish))
    wait(number, store_sem)


def parts_of(n_chip):
    far = n_chip // 2
    near = [s for s in range(n_chip) if s != far]
    return [near] * CORES, [[far]] * CORES


def block_of(out_ref, tile, per_col, width):
    rows = pl.ds(pl.multiple_of(lax.div(tile, per_col) * width, width), width)
    columns = pl.ds(pl.multiple_of(lax.rem(tile, per_col) * width, width), width)
    return out_ref.at[rows, columns]


def main_kernel(n_row, n_chip, slots, per_row, per_col, pieces, *refs):
    early, late = parts_of(n_chip)
    n_left = sum(map(len, early))
    n_source = n_left + len(pieces)
    sources = refs[:n_source]
    out_ref, right_ref, plan = refs[n_source + 1 :][:3]
    acc, left_buf, right_buf, fact_buf, code_buf = refs[n_source + 4 :][:5]
    load_sem, code_sem, store_sem = refs[n_source + 9 :]
    r = lax.axis_index("row")
    c = lax.axis_index("col")
    z, core = lax.div(c, CORES), lax.rem(c, CORES)
    rows, width = left_buf.shape[-1], acc.shape[-1]
    tiles = per_row * per_col
    stations = CORES * n_row * n_chip

    def load(index):
        if index < n_left:
            target = left_buf.at[index]
            source = sources[index].at[pl.ds(0, target.shape[0])]
        else:
            which, first, number = pieces[index - n_left]
            target = right_buf.at[which, pl.ds(first, number)]
            source = sources[index]
        return pltpu.make_async_copy(source, target, load_sem.at[index])

    for index in [*range(n_left, n_source), *range(n_left)]:
        load(index).start()
    for index, (which, first, number) in enumerate(pieces):
        load(n_left + index).wait()
        for s in range(first, first + number):
            station = which * n_chip + s
            meta = right_buf[which, s, slots * rows :].astype(jnp.float32)
            for i in range(slots + 1):
                fact_buf[i, station : station + 1, :] = meta[i : i + 1]
    code, tile_row = plan_of(
        fact_buf, r, z, core, n_row, n_chip, slots, per_col, tiles, acc.shape[0] > tiles
    )
    code_buf[0:1, :] = code
    code_buf[1:2, :] = tile_row
    to_smem = pltpu.make_async_copy(code_buf, plan, code_sem)
    to_smem.start()
    kept = 0
    for other in range(CORES):
        for j in range(n_row):
            for s in late[other]:
                right_ref[kept] = right_buf[other * n_row + j, s, : slots * rows]
                kept += 1
    for index in range(n_left):
        load(index).wait()
    to_smem.wait()

    def group(other):
        base = len(early[0]) * other

        def stations_of(j):
            index = other * n_row + j

            def station(m, s):
                def left():
                    return left_buf[base + m, pl.ds(j * slots * width, slots * width)]

                def right():
                    tiles = [right_buf[index, s, i * rows : (i + 1) * rows] for i in range(slots)]
                    return jnp.concatenate(tiles, axis=1)

                return index * n_chip + s, left, right

            return [station(m, s) for m, s in enumerate(early[other])]

        return n_row, stations_of

    groups = [group(other) for other in range(CORES)]
    settle(plan, groups, stations, slots, acc, None, out_ref, per_col, None, store_sem)


def main_part(left, right, pieces, out, n_row, per_row, per_col):
    n_chip = len(left[0]) + 1
    early, late = parts_of(n_chip)
    flat = [*left[0], *left[1]]
    rows, width = flat[0].shape[1], right[0].shape[2]
    slots = right[0].shape[1] // rows
    height = n_row * slots * width
    tiles = per_row * per_col
    stations = CORES * n_row * n_chip
    pairs = slots * slots * stations
    places = min(tiles + 1, pairs)
    plan = (8, pairs)
    sources = [*flat, *right]
    anywhere = pl.BlockSpec(memory_space=pl.ANY)
    held = (
        places * width * width * 4
        + len(flat) * height * rows * 2
        + (stations + n_row * sum(map(len, late))) * (slots * rows + META) * width * 2
        + (slots + 1) * stations * width * 4
        + 8 * pairs * pairs * 4
    )
    return pl.pallas_call(
        functools.partial(main_kernel, n_row, n_chip, slots, per_row, per_col, pieces),
        out_shape=[
            jax.ShapeDtypeStruct(out.shape, out.dtype),
            jax.ShapeDtypeStruct(
                (n_row * sum(map(len, late)), slots * rows, width), jnp.bfloat16
            ),
            jax.ShapeDtypeStruct(plan, jnp.int32),
        ],
        in_specs=[anywhere] * (len(sources) + 1),
        out_specs=[
            anywhere,
            pl.BlockSpec(memory_space=pltpu.VMEM),
            pl.BlockSpec(memory_space=pltpu.SMEM),
        ],
        scratch_shapes=[
            pltpu.VMEM((places, width, width), jnp.float32),
            pltpu.VMEM((len(flat), height, rows), jnp.bfloat16),
            pltpu.VMEM((CORES * n_row, n_chip, slots * rows + META, width), jnp.bfloat16),
            pltpu.VMEM((slots + 1, stations, width), jnp.float32),
            pltpu.VMEM(plan, jnp.int32),
            pltpu.SemaphoreType.DMA((len(sources),)),
            pltpu.SemaphoreType.DMA,
            pltpu.SemaphoreType.DMA,
        ],
        input_output_aliases={len(sources): 0},
        compiler_params=pltpu.CompilerParams(vmem_limit_bytes=held + 3 * MIB),
        cost_estimate=pl.CostEstimate(flops=0, bytes_accessed=0, transcendentals=0),
    )(*sources, out)


def tail_kernel(n_row, n_chip, slots, per_col, plan, *refs):
    _, late = parts_of(n_chip)
    n_left = sum(map(len, late))
    lefts, right_ref = refs[:n_left], refs[n_left]
    out_ref, acc, held, load_sem, store_sem = refs[n_left + 2 :]
    rows, width = lefts[0].shape[-1], acc.shape[-1]
    stations = CORES * n_row * n_chip

    found = []
    for other in range(CORES):
        for j in range(n_row):
            for m, s in enumerate(late[other]):
                source = lefts[len(late[0]) * other + m]

                def left(source=source, j=j):
                    return source[j * slots * width : (j + 1) * slots * width]

                def right(kept=len(found)):
                    tiles = [right_ref[kept, i * rows : (i + 1) * rows] for i in range(slots)]
                    return jnp.concatenate(tiles, axis=1)

                found.append(((other * n_row + j) * n_chip + s, left, right))
    groups = [(1, lambda step: found)]
    settle(plan, groups, stations, slots, acc, held, out_ref, per_col, load_sem, store_sem)


def tail_part(left, right, plan, out, n_row, per_row, per_col):
    flat = [*left[0], *left[1]]
    _, depth, width = right.shape
    slots = depth // flat[0].shape[1]
    stations = plan.shape[1] // slots**2
    n_chip = stations // (CORES * n_row)
    places = (min(per_row * per_col + 1, plan.shape[1]), width, width)
    anywhere = pl.BlockSpec(memory_space=pl.ANY)
    vmem = pl.BlockSpec(memory_space=pltpu.VMEM)
    smem = pl.BlockSpec(memory_space=pltpu.SMEM)
    held = 2 * places[0] * width * width * 4 + 2 * right.size * 2 + 2 * MIB * len(flat)
    return pl.pallas_call(
        functools.partial(tail_kernel, n_row, n_chip, slots, per_col),
        out_shape=jax.ShapeDtypeStruct(out.shape, out.dtype),
        in_specs=[smem] + [vmem] * (len(flat) + 1) + [anywhere],
        out_specs=anywhere,
        scratch_shapes=[
            pltpu.VMEM(places, jnp.float32),
            pltpu.VMEM(places, jnp.float32),
            pltpu.SemaphoreType.DMA,
            pltpu.SemaphoreType.DMA,
        ],
        input_output_aliases={len(flat) + 2: 0},
        compiler_params=pltpu.CompilerParams(vmem_limit_bytes=held + 4 * MIB),
        cost_estimate=pl.CostEstimate(flops=0, bytes_accessed=0, transcendentals=0),
    )(plan, *flat, right, out)


def zero_kernel(first, count, *refs):
    out_ref, block, sem = refs[-3:]
    block[...] = jnp.zeros_like(block)
    height = block.shape[0]
    copies = [
        pltpu.make_async_copy(block, out_ref.at[pl.ds((first + n) * height, height)], sem.at[n])
        for n in range(count)
    ]
    for copy in copies:
        copy.start()
    for copy in copies:
        copy.wait()


def zero_part(height, width, part, after, out=None):
    step = 128
    count = height // step
    early = count * ZERO_EARLY // 16
    first, number = ((0, early), (early, count - early))[part]
    anywhere = pl.BlockSpec(memory_space=pl.ANY)
    inputs = [after] if out is None else [after, out]
    return pl.pallas_call(
        functools.partial(zero_kernel, first, number),
        out_shape=jax.ShapeDtypeStruct((height, width), jnp.float32),
        in_specs=[anywhere] * len(inputs),
        out_specs=anywhere,
        scratch_shapes=[
            pltpu.VMEM((step, width), jnp.float32),
            pltpu.SemaphoreType.DMA((number,)),
        ],
        input_output_aliases={} if out is None else {1: 0},
        compiler_params=pltpu.CompilerParams(vmem_limit_bytes=4 * MIB),
        cost_estimate=pl.CostEstimate(
            flops=0, bytes_accessed=height * width * 2, transcendentals=0
        ),
    )(*inputs)


def local(sensitivity, tile_ids, counts, weight_class):
    n_row = lax.axis_size("row")
    n_col = lax.axis_size("col")
    n_chip = n_col // CORES
    width = sensitivity.shape[-1]
    per_row = TILES // n_row
    per_col = TILES // n_col
    middle = n_chip // 2

    def flip_row(value, j):
        return lax.ppermute(value, "row", [(i, i ^ j) for i in range(n_row)])

    def shift_chip(value, s):
        pairs = [(i, (i + CORES * s) % n_col) for i in range(n_col)]
        return lax.ppermute(value, "col", pairs)

    def flip_core(value):
        return lax.ppermute(value, "col", [(i, i ^ 1) for i in range(n_col)])

    def pad(value, extra):
        return jnp.pad(value, ((0, extra), (0, 0)))

    after = lax.optimization_barrier

    ids = jnp.transpose(tile_ids, (0, 2, 1))[0]
    parts = pack(sensitivity[0], weight_class, ids, counts, n_chip)
    to_row, to_chip = parts[:n_row], parts[n_row:]
    plane = [to_row[0]] + [flip_row(to_row[j], j) for j in range(1, n_row)]
    from_chip = [to_chip[0]] + [shift_chip(to_chip[s], s) for s in range(1, n_chip)]
    height, breadth = per_row * width, per_col * width
    zeros = zero_part(height, breadth, 0, to_chip[0])
    plane, from_chip, zeros = after((plane, from_chip, zeros))
    rows = sensitivity.shape[-2]
    chip = jnp.stack(plane).reshape(-1, rows)
    near = {0: chip}
    for s in range(1, middle):
        near[s] = shift_chip(near[s - 1], 1)
        near[n_chip - s] = shift_chip(pad(chip, 32) if s == 1 else near[n_chip - s + 1], -1)
    right = jnp.stack(from_chip)
    own = [flip_core(chip), flip_core(right)]
    *own, again, token = after((*own, right, to_chip[0]))
    sides = [right] + [flip_row(right if j == 1 else again, j) for j in range(1, n_row)]
    far = shift_chip(pad(near[middle - 1], 48), 1)
    swapped = {s: flip_core(near[s]) for s in range(1, middle)}
    zeros = zero_part(height, breadth, 1, token, zeros)
    swapped, waiting, zeros = after((swapped, sides[1:], zeros))
    swapped |= {s: flip_core(near[s]) for s in near if s > middle} | {0: own[0]}
    sides += [own[1]] + [flip_core(x) for x in waiting]
    pieces = [(index, 0, n_chip) for index in range(CORES * n_row)]
    early = [[near[s] for s in sorted(near)], [swapped[s] for s in sorted(swapped)]]
    out, tail_right, plan = main_part(early, sides, pieces, zeros, n_row, per_row, per_col)
    far, plan = after((far, plan))
    return tail_part([[far], [flip_core(far)]], tail_right, plan, out, n_row, per_row, per_col)


def solution(mesh):
    in_specs = (
        P(("row", "col"), None, None, None, None),
        P(("row", "col"), None, None),
        P(("row", "col"), None),
        P(("row", "col"), None),
    )
    return jax.shard_map(
        local, mesh=mesh, in_specs=in_specs, out_specs=P("row", "col"), check_vma=False
    )
```

```python
import functools

import jax
import jax.numpy as jnp
from jax import lax
from jax.experimental import pallas as pl
from jax.experimental.pallas import tpu as pltpu
from jax.sharding import PartitionSpec as P

TILES = 128
CORES = 2
META = 16
ZERO_EARLY = 6
MIB = 1024 * 1024


def scale_of(class_ref):
    classes = class_ref[...]
    return jnp.where(
        classes == 0, 1.0, jnp.where(classes == 1, 0.5, jnp.where(classes == 2, 0.25, 0.125))
    ).astype(jnp.float32)


def pack_kernel(n_row, n_chip, slots, sens_ref, class_ref, ids_ref, counts_ref, *refs):
    outs, meta_ref = refs[:-1], refs[-1]
    r = lax.axis_index("row")
    z = lax.div(lax.axis_index("col"), CORES)
    rows, width = sens_ref.shape[2:]
    scale = scale_of(class_ref)
    for j in range(n_row):
        for i in range(slots):
            tile = sens_ref[r ^ j, i].T.astype(jnp.float32) * scale
            outs[j][i * width : (i + 1) * width] = tile.astype(jnp.bfloat16)
    scale = jnp.broadcast_to(scale, (width, rows)).T
    meta_ref[...] = jnp.zeros_like(meta_ref)
    meta_ref[:slots, :n_row] = ids_ref[...].astype(jnp.float32)
    meta_ref[slots : slots + 1, :n_row] = counts_ref[...].astype(jnp.float32)
    meta = meta_ref[...].astype(jnp.bfloat16)
    for s in range(n_chip):
        owner = lax.rem(z + s, n_chip)
        out = outs[n_row + s]
        for i in range(slots):
            tile = sens_ref[owner, i].astype(jnp.float32) * scale
            out[i * rows : (i + 1) * rows] = tile.astype(jnp.bfloat16)
        out[slots * rows :] = meta


def pack(sensitivity, weight_class, ids, counts, n_chip):
    n_row, slots, rows, width = sensitivity.shape
    vmem = pl.BlockSpec(memory_space=pltpu.VMEM)
    return pl.pallas_call(
        functools.partial(pack_kernel, n_row, n_chip, slots),
        out_shape=[jax.ShapeDtypeStruct((slots * width, rows), jnp.bfloat16)] * n_row
        + [jax.ShapeDtypeStruct((slots * rows + META, width), jnp.bfloat16)] * n_chip,
        in_specs=[vmem] * 4,
        out_specs=[vmem] * (n_row + n_chip),
        scratch_shapes=[pltpu.VMEM((META, width), jnp.float32)],
        cost_estimate=pl.CostEstimate(flops=0, bytes_accessed=0, transcendentals=0),
    )(sensitivity, weight_class, ids, counts)


def plan_of(facts, r, z, core, n_row, n_chip, slots, per_col, none, by_tile):
    _, stations, width = facts.shape
    lane = lax.broadcasted_iota(jnp.int32, (stations, width), 1)

    def pick(row, owner):
        return jnp.sum(jnp.where(lane == owner, facts[row], 0.0), axis=1, keepdims=True)

    used_left, used_right = pick(slots, r), pick(slots, z)
    lefts = [pick(i, r) for i in range(slots)]
    rights = [pick(j, z) - (core * per_col).astype(jnp.float32) for j in range(slots)]
    column = []
    for i in range(slots):
        for j in range(slots):
            met = (i < used_left) & (j < used_right) & (rights[j] >= 0) & (rights[j] < per_col)
            column.append(jnp.where(met, lefts[i] * per_col + rights[j], float(none)))
    count = len(column) * stations
    tile = jnp.broadcast_to(jnp.concatenate(column, axis=0), (count, count))
    other = tile.T

    def part_of(axis):
        pair = lax.broadcasted_iota(jnp.int32, (count, count), axis)
        station = lax.rem(pair, stations)
        s = lax.rem(station, n_chip)
        tail = s == n_chip // 2
        number = jnp.where(tail, lax.div(station, n_chip), station) * len(column)
        return tail, (number + lax.div(pair, stations)).astype(jnp.float32)

    tail_down, number_down = part_of(0)
    tail_across, number_across = part_of(1)
    same = (tile == other) & (tail_down == tail_across)
    first = jnp.min(jnp.where(same, number_down, 1e6), axis=0, keepdims=True)
    fresh = (first == number_across[:1]).astype(jnp.float32)
    last = jnp.max(jnp.where(same, number_down, -1.0), axis=0, keepdims=True)
    final = (last == number_across[:1]).astype(jnp.float32)
    real = (other[:1] < none).astype(jnp.float32)
    place = other[:1] if by_tile else first
    met = (tile == other) & jnp.logical_not(tail_down)
    met = jnp.min(jnp.where(met, number_down, 1e6), axis=0, keepdims=True)
    before = jnp.where(met < 1e6, other[:1] if by_tile else met, -1.0)
    code = 8.0 * place + 4.0 * final * real + 2.0 * fresh * real + fresh
    return [row.astype(jnp.int32) for row in (code, other[:1], before)]


def each_hit(plan, columns, flag, act):
    number = 0
    for column in columns:
        code = plan[0, column]
        hit = lax.shift_right_logical(code, flag) & 1

        @pl.when(hit == 1)
        def _():
            act(lax.shift_right_logical(code, 3), column)

        number = number + hit
    return number


def settle(plan, groups, stations, slots, acc, base, out_ref, per_col, store_sem):
    width = acc.shape[-1]
    pairs = slots * slots

    def store(place, column):
        block = block_of(out_ref, plan[1, column], per_col, width)
        pltpu.make_async_copy(acc.at[place], block, store_sem).start()

    def add(column, left, right):
        gram = jnp.dot(left(), right(), preferred_element_type=jnp.float32)
        for n in range(pairs):
            code = plan[0, column + n * stations]
            place, fresh = lax.shift_right_logical(code, 3), code & 1
            i, j = divmod(n, slots)
            part = gram[i * width : (i + 1) * width, j * width : (j + 1) * width]
            start = part if base is None else base[place] + part
            acc[place] = jnp.where(fresh == 1, start, acc[place] + part)

    def add_store(found):
        for column, left, right in found:
            add(column, left, right)
        columns = [column + n * stations for column, _, _ in found for n in range(pairs)]
        return each_hit(plan, columns, 2, store)

    total = 0
    for steps, stations_of in groups:
        if steps == 1:
            total = total + add_store(stations_of(0))
        else:
            total = lax.fori_loop(
                0, steps, lambda step, sofar: sofar + add_store(stations_of(step)), total
            )
    return total


def drain(number, acc, sem):
    def step(index, carry):
        pltpu.make_async_copy(acc.at[0], acc.at[0], sem).wait()
        return carry

    lax.fori_loop(0, number, step, 0)


def parts_of(n_chip):
    far = n_chip // 2
    near = [s for s in range(n_chip) if s != far]
    return [near] * CORES, [[far]] * CORES


def block_of(out_ref, tile, per_col, width):
    rows = pl.ds(pl.multiple_of(lax.div(tile, per_col) * width, width), width)
    columns = pl.ds(pl.multiple_of(lax.rem(tile, per_col) * width, width), width)
    return out_ref.at[rows, columns]


def main_kernel(n_row, n_chip, slots, per_row, per_col, pieces, *refs):
    early, late = parts_of(n_chip)
    n_left = sum(map(len, early))
    n_source = n_left + len(pieces)
    sources = refs[:n_source]
    out_ref, right_ref, carry_ref, plan = refs[n_source + 1 :][:4]
    acc, left_buf, right_buf, fact_buf, code_buf = refs[n_source + 5 :][:5]
    load_sem, code_sem, store_sem = refs[n_source + 10 :]
    r = lax.axis_index("row")
    c = lax.axis_index("col")
    z, core = lax.div(c, CORES), lax.rem(c, CORES)
    rows, width = left_buf.shape[-1], acc.shape[-1]
    tiles = per_row * per_col
    stations = CORES * n_row * n_chip

    def load(index):
        if index < n_left:
            target = left_buf.at[index]
            source = sources[index].at[pl.ds(0, target.shape[0])]
        else:
            which, first, number = pieces[index - n_left]
            target = right_buf.at[which, pl.ds(first, number)]
            source = sources[index]
        return pltpu.make_async_copy(source, target, load_sem.at[index])

    for index in [*range(n_left, n_source), *range(n_left)]:
        load(index).start()
    for index, (which, first, number) in enumerate(pieces):
        load(n_left + index).wait()
        for s in range(first, first + number):
            station = which * n_chip + s
            meta = right_buf[which, s, slots * rows :].astype(jnp.float32)
            for i in range(slots + 1):
                fact_buf[i, station : station + 1, :] = meta[i : i + 1]
    by_tile = acc.shape[0] > tiles
    lines = plan_of(fact_buf, r, z, core, n_row, n_chip, slots, per_col, tiles, by_tile)
    for n, line in enumerate(lines):
        code_buf[n : n + 1, :] = line
    to_smem = pltpu.make_async_copy(code_buf, plan, code_sem)
    to_smem.start()
    kept = 0
    for other in range(CORES):
        for j in range(n_row):
            for s in late[other]:
                right_ref[kept] = right_buf[other * n_row + j, s, : slots * rows]
                kept += 1
    for index in range(n_left):
        load(index).wait()
    to_smem.wait()

    def group(other):
        base = len(early[0]) * other

        def stations_of(j):
            index = other * n_row + j

            def station(m, s):
                def left():
                    return left_buf[base + m, pl.ds(j * slots * width, slots * width)]

                def right():
                    tiles = [right_buf[index, s, i * rows : (i + 1) * rows] for i in range(slots)]
                    return jnp.concatenate(tiles, axis=1)

                return index * n_chip + s, left, right

            return [station(m, s) for m, s in enumerate(early[other])]

        return n_row, stations_of

    groups = [group(other) for other in range(CORES)]
    number = settle(plan, groups, stations, slots, acc, None, out_ref, per_col, store_sem)

    def hand_on(place, column):
        before = plan[2, column]
        carry_ref[place] = jnp.where(before < 0, 0.0, acc[jnp.maximum(before, 0)])

    def hand_step(index, carry):
        column = index * n_chip + n_chip // 2
        each_hit(plan, [column + n * stations for n in range(slots * slots)], 1, hand_on)
        return carry

    lax.fori_loop(0, CORES * n_row, hand_step, 0)
    drain(number, acc, store_sem)


def main_part(left, right, pieces, out, n_row, per_row, per_col):
    n_chip = len(left[0]) + 1
    early, late = parts_of(n_chip)
    flat = [*left[0], *left[1]]
    rows, width = flat[0].shape[1], right[0].shape[2]
    slots = right[0].shape[1] // rows
    height = n_row * slots * width
    tiles = per_row * per_col
    stations = CORES * n_row * n_chip
    pairs = slots * slots * stations
    places = min(tiles + 1, pairs)
    by_tile = places > tiles
    tail_places = (places if by_tile else slots * slots * CORES * n_row, width, width)
    plan = (8, pairs)
    sources = [*flat, *right]
    anywhere = pl.BlockSpec(memory_space=pl.ANY)
    held = (
        (places + tail_places[0]) * width * width * 4
        + len(flat) * height * rows * 2
        + (stations + n_row * sum(map(len, late))) * (slots * rows + META) * width * 2
        + (slots + 1) * stations * width * 4
        + 8 * pairs * pairs * 4
    )
    return pl.pallas_call(
        functools.partial(main_kernel, n_row, n_chip, slots, per_row, per_col, pieces),
        out_shape=[
            jax.ShapeDtypeStruct(out.shape, out.dtype),
            jax.ShapeDtypeStruct(
                (n_row * sum(map(len, late)), slots * rows, width), jnp.bfloat16
            ),
            jax.ShapeDtypeStruct(tail_places, jnp.float32),
            jax.ShapeDtypeStruct(plan, jnp.int32),
        ],
        in_specs=[anywhere] * (len(sources) + 1),
        out_specs=[
            anywhere,
            pl.BlockSpec(memory_space=pltpu.VMEM),
            pl.BlockSpec(memory_space=pltpu.VMEM),
            pl.BlockSpec(memory_space=pltpu.SMEM),
        ],
        scratch_shapes=[
            pltpu.VMEM((places, width, width), jnp.float32),
            pltpu.VMEM((len(flat), height, rows), jnp.bfloat16),
            pltpu.VMEM((CORES * n_row, n_chip, slots * rows + META, width), jnp.bfloat16),
            pltpu.VMEM((slots + 1, stations, width), jnp.float32),
            pltpu.VMEM(plan, jnp.int32),
            pltpu.SemaphoreType.DMA((len(sources),)),
            pltpu.SemaphoreType.DMA,
            pltpu.SemaphoreType.DMA,
        ],
        input_output_aliases={len(sources): 0},
        compiler_params=pltpu.CompilerParams(vmem_limit_bytes=held + 3 * MIB),
        cost_estimate=pl.CostEstimate(flops=0, bytes_accessed=0, transcendentals=0),
    )(*sources, out)


def tail_kernel(n_row, n_chip, slots, per_col, plan, *refs):
    _, late = parts_of(n_chip)
    n_left = sum(map(len, late))
    lefts, right_ref, base_ref = refs[:n_left], refs[n_left], refs[n_left + 1]
    out_ref, acc, store_sem = refs[n_left + 3 :]
    rows, width = lefts[0].shape[-1], acc.shape[-1]
    stations = CORES * n_row * n_chip

    found = []
    for other in range(CORES):
        for j in range(n_row):
            for m, s in enumerate(late[other]):
                source = lefts[len(late[0]) * other + m]

                def left(source=source, j=j):
                    return source[j * slots * width : (j + 1) * slots * width]

                def right(kept=len(found)):
                    tiles = [right_ref[kept, i * rows : (i + 1) * rows] for i in range(slots)]
                    return jnp.concatenate(tiles, axis=1)

                found.append(((other * n_row + j) * n_chip + s, left, right))
    groups = [(1, lambda step: found)]
    number = settle(plan, groups, stations, slots, acc, base_ref, out_ref, per_col, store_sem)
    drain(number, acc, store_sem)


def tail_part(left, right, base, plan, out, n_row, per_row, per_col):
    flat = [*left[0], *left[1]]
    _, depth, width = right.shape
    slots = depth // flat[0].shape[1]
    stations = plan.shape[1] // slots**2
    n_chip = stations // (CORES * n_row)
    anywhere = pl.BlockSpec(memory_space=pl.ANY)
    vmem = pl.BlockSpec(memory_space=pltpu.VMEM)
    smem = pl.BlockSpec(memory_space=pltpu.SMEM)
    held = 3 * base.size * 4 + 2 * right.size * 2 + 2 * MIB * len(flat)
    return pl.pallas_call(
        functools.partial(tail_kernel, n_row, n_chip, slots, per_col),
        out_shape=jax.ShapeDtypeStruct(out.shape, out.dtype),
        in_specs=[smem] + [vmem] * (len(flat) + 2) + [anywhere],
        out_specs=anywhere,
        scratch_shapes=[
            pltpu.VMEM(base.shape, jnp.float32),
            pltpu.SemaphoreType.DMA,
        ],
        input_output_aliases={len(flat) + 3: 0},
        compiler_params=pltpu.CompilerParams(vmem_limit_bytes=held + 4 * MIB),
        cost_estimate=pl.CostEstimate(flops=0, bytes_accessed=0, transcendentals=0),
    )(plan, *flat, right, base, out)


def zero_kernel(first, count, *refs):
    out_ref, block, sem = refs[-3:]
    block[...] = jnp.zeros_like(block)
    height = block.shape[0]
    copies = [
        pltpu.make_async_copy(block, out_ref.at[pl.ds((first + n) * height, height)], sem.at[n])
        for n in range(count)
    ]
    for copy in copies:
        copy.start()
    for copy in copies:
        copy.wait()


def zero_part(height, width, part, after, out=None):
    step = 128
    count = height // step
    early = count * ZERO_EARLY // 16
    first, number = ((0, early), (early, count - early))[part]
    anywhere = pl.BlockSpec(memory_space=pl.ANY)
    inputs = [after] if out is None else [after, out]
    return pl.pallas_call(
        functools.partial(zero_kernel, first, number),
        out_shape=jax.ShapeDtypeStruct((height, width), jnp.float32),
        in_specs=[anywhere] * len(inputs),
        out_specs=anywhere,
        scratch_shapes=[
            pltpu.VMEM((step, width), jnp.float32),
            pltpu.SemaphoreType.DMA((number,)),
        ],
        input_output_aliases={} if out is None else {1: 0},
        compiler_params=pltpu.CompilerParams(vmem_limit_bytes=4 * MIB),
        cost_estimate=pl.CostEstimate(
            flops=0, bytes_accessed=height * width * 2, transcendentals=0
        ),
    )(*inputs)


def local(sensitivity, tile_ids, counts, weight_class):
    n_row = lax.axis_size("row")
    n_col = lax.axis_size("col")
    n_chip = n_col // CORES
    width = sensitivity.shape[-1]
    per_row = TILES // n_row
    per_col = TILES // n_col
    middle = n_chip // 2

    def flip_row(value, j):
        return lax.ppermute(value, "row", [(i, i ^ j) for i in range(n_row)])

    def shift_chip(value, s):
        pairs = [(i, (i + CORES * s) % n_col) for i in range(n_col)]
        return lax.ppermute(value, "col", pairs)

    def flip_core(value):
        return lax.ppermute(value, "col", [(i, i ^ 1) for i in range(n_col)])

    def pad(value, extra):
        return jnp.pad(value, ((0, extra), (0, 0)))

    after = lax.optimization_barrier

    ids = jnp.transpose(tile_ids, (0, 2, 1))[0]
    parts = pack(sensitivity[0], weight_class, ids, counts, n_chip)
    to_row, to_chip = parts[:n_row], parts[n_row:]
    plane = [to_row[0]] + [flip_row(to_row[j], j) for j in range(1, n_row)]
    from_chip = [to_chip[0]] + [shift_chip(to_chip[s], s) for s in range(1, n_chip)]
    height, breadth = per_row * width, per_col * width
    zeros = zero_part(height, breadth, 0, to_chip[0])
    plane, from_chip, zeros = after((plane, from_chip, zeros))
    rows = sensitivity.shape[-2]
    chip = jnp.stack(plane).reshape(-1, rows)
    near = {0: chip}
    for s in range(1, middle):
        near[s] = shift_chip(near[s - 1], 1)
        near[n_chip - s] = shift_chip(pad(chip, 32) if s == 1 else near[n_chip - s + 1], -1)
    right = jnp.stack(from_chip)
    own = [flip_core(chip), flip_core(right)]
    *own, again, token = after((*own, right, to_chip[0]))
    sides = [right] + [flip_row(right if j == 1 else again, j) for j in range(1, n_row)]
    far = shift_chip(pad(near[middle - 1], 48), 1)
    swapped = {s: flip_core(near[s]) for s in range(1, middle)}
    zeros = zero_part(height, breadth, 1, token, zeros)
    swapped, waiting, zeros = after((swapped, sides[1:], zeros))
    swapped |= {s: flip_core(near[s]) for s in near if s > middle} | {0: own[0]}
    sides += [own[1]] + [flip_core(x) for x in waiting]
    pieces = [(index, 0, n_chip) for index in range(CORES * n_row)]
    early = [[near[s] for s in sorted(near)], [swapped[s] for s in sorted(swapped)]]
    out, tail_right, base, plan = main_part(early, sides, pieces, zeros, n_row, per_row, per_col)
    far, plan = after((far, plan))
    return tail_part(
        [[far], [flip_core(far)]], tail_right, base, plan, out, n_row, per_row, per_col
    )


def solution(mesh):
    in_specs = (
        P(("row", "col"), None, None, None, None),
        P(("row", "col"), None, None),
        P(("row", "col"), None),
        P(("row", "col"), None),
    )
    return jax.shard_map(
        local, mesh=mesh, in_specs=in_specs, out_specs=P("row", "col"), check_vma=False
    )
```

```python
import functools

import jax
import jax.numpy as jnp
from jax import lax
from jax.experimental import pallas as pl
from jax.experimental.pallas import tpu as pltpu
from jax.sharding import PartitionSpec as P

TILES = 128
CORES = 2
META = 16
ZERO_EARLY = 6
MIB = 1024 * 1024


def scale_of(class_ref):
    classes = class_ref[...]
    return jnp.where(
        classes == 0, 1.0, jnp.where(classes == 1, 0.5, jnp.where(classes == 2, 0.25, 0.125))
    ).astype(jnp.float32)


def pack_kernel(n_row, n_chip, slots, sens_ref, class_ref, ids_ref, counts_ref, *refs):
    outs, meta_ref = refs[:-1], refs[-1]
    r = lax.axis_index("row")
    z = lax.div(lax.axis_index("col"), CORES)
    rows, width = sens_ref.shape[2:]
    scale = scale_of(class_ref)
    for j in range(n_row):
        for i in range(slots):
            tile = sens_ref[r ^ j, i].T.astype(jnp.float32) * scale
            outs[j][i * width : (i + 1) * width] = tile.astype(jnp.bfloat16)
    scale = jnp.broadcast_to(scale, (width, rows)).T
    meta_ref[...] = jnp.zeros_like(meta_ref)
    meta_ref[:slots, :n_row] = ids_ref[...].astype(jnp.float32)
    meta_ref[slots : slots + 1, :n_row] = counts_ref[...].astype(jnp.float32)
    meta = meta_ref[...].astype(jnp.bfloat16)
    for s in range(n_chip):
        owner = lax.rem(z + s, n_chip)
        out = outs[n_row + s]
        for i in range(slots):
            tile = sens_ref[owner, i].astype(jnp.float32) * scale
            out[i * rows : (i + 1) * rows] = tile.astype(jnp.bfloat16)
        out[slots * rows :] = meta


def pack(sensitivity, weight_class, ids, counts, n_chip):
    n_row, slots, rows, width = sensitivity.shape
    vmem = pl.BlockSpec(memory_space=pltpu.VMEM)
    return pl.pallas_call(
        functools.partial(pack_kernel, n_row, n_chip, slots),
        out_shape=[jax.ShapeDtypeStruct((slots * width, rows), jnp.bfloat16)] * n_row
        + [jax.ShapeDtypeStruct((slots * rows + META, width), jnp.bfloat16)] * n_chip,
        in_specs=[vmem] * 4,
        out_specs=[vmem] * (n_row + n_chip),
        scratch_shapes=[pltpu.VMEM((META, width), jnp.float32)],
        cost_estimate=pl.CostEstimate(flops=0, bytes_accessed=0, transcendentals=0),
    )(sensitivity, weight_class, ids, counts)


def plan_of(facts, r, z, core, n_row, n_chip, slots, per_col, none, by_tile):
    _, stations, width = facts.shape
    lane = lax.broadcasted_iota(jnp.int32, (stations, width), 1)

    def pick(row, owner):
        return jnp.sum(jnp.where(lane == owner, facts[row], 0.0), axis=1, keepdims=True)

    used_left, used_right = pick(slots, r), pick(slots, z)
    lefts = [pick(i, r) for i in range(slots)]
    rights = [pick(j, z) - (core * per_col).astype(jnp.float32) for j in range(slots)]
    column = []
    for i in range(slots):
        for j in range(slots):
            met = (i < used_left) & (j < used_right) & (rights[j] >= 0) & (rights[j] < per_col)
            column.append(jnp.where(met, lefts[i] * per_col + rights[j], float(none)))
    count = len(column) * stations
    tile = jnp.broadcast_to(jnp.concatenate(column, axis=0), (count, count))
    other = tile.T

    def part_of(axis):
        pair = lax.broadcasted_iota(jnp.int32, (count, count), axis)
        station = lax.rem(pair, stations)
        s = lax.rem(station, n_chip)
        tail = s == n_chip // 2
        number = jnp.where(tail, lax.div(station, n_chip), station) * len(column)
        return tail, (number + lax.div(pair, stations)).astype(jnp.float32)

    tail_down, number_down = part_of(0)
    tail_across, number_across = part_of(1)
    same = (tile == other) & (tail_down == tail_across)
    first = jnp.min(jnp.where(same, number_down, 1e6), axis=0, keepdims=True)
    fresh = (first == number_across[:1]).astype(jnp.float32)
    last = jnp.max(jnp.where(same, number_down, -1.0), axis=0, keepdims=True)
    final = (last == number_across[:1]).astype(jnp.float32)
    real = (other[:1] < none).astype(jnp.float32)
    place = other[:1] if by_tile else first
    met = (tile == other) & jnp.logical_not(tail_down)
    met = jnp.min(jnp.where(met, number_down, 1e6), axis=0, keepdims=True)
    before = jnp.where(met < 1e6, other[:1] if by_tile else met, -1.0)
    code = 8.0 * place + 4.0 * final * real + 2.0 * fresh * real + fresh
    return [row.astype(jnp.int32) for row in (code, other[:1], before)]


def each_hit(plan, columns, flag, act):
    number = 0
    for column in columns:
        code = plan[0, column]
        hit = lax.shift_right_logical(code, flag) & 1

        @pl.when(hit == 1)
        def _():
            act(lax.shift_right_logical(code, 3), column)

        number = number + hit
    return number


def settle(plan, groups, stations, slots, acc, base, out_ref, per_col, store_sem):
    width = acc.shape[-1]
    pairs = slots * slots

    def store(place, column):
        block = block_of(out_ref, plan[1, column], per_col, width)
        pltpu.make_async_copy(acc.at[place], block, store_sem).start()

    def add(column, left, right):
        gram = jnp.dot(left(), right(), preferred_element_type=jnp.float32)
        for n in range(pairs):
            code = plan[0, column + n * stations]
            place, fresh = lax.shift_right_logical(code, 3), code & 1
            i, j = divmod(n, slots)
            part = gram[i * width : (i + 1) * width, j * width : (j + 1) * width]
            start = part if base is None else base[place] + part
            acc[place] = jnp.where(fresh == 1, start, acc[place] + part)

    def add_store(found):
        for column, left, right in found:
            add(column, left, right)
        columns = [column + n * stations for column, _, _ in found for n in range(pairs)]
        return each_hit(plan, columns, 2, store)

    total = 0
    for steps, stations_of in groups:
        if steps == 1:
            total = total + add_store(stations_of(0))
        else:
            total = lax.fori_loop(
                0, steps, lambda step, sofar: sofar + add_store(stations_of(step)), total
            )
    return total


def drain(number, acc, sem):
    def step(index, carry):
        pltpu.make_async_copy(acc.at[0], acc.at[0], sem).wait()
        return carry

    lax.fori_loop(0, number, step, 0)


def parts_of(n_chip):
    far = n_chip // 2
    near = [s for s in range(n_chip) if s != far]
    return [near] * CORES, [[far]] * CORES


def block_of(out_ref, tile, per_col, width):
    rows = pl.ds(pl.multiple_of(lax.div(tile, per_col) * width, width), width)
    columns = pl.ds(pl.multiple_of(lax.rem(tile, per_col) * width, width), width)
    return out_ref.at[rows, columns]


def main_kernel(n_row, n_chip, slots, per_row, per_col, *refs):
    early, late = parts_of(n_chip)
    n_left = sum(map(len, early))
    n_source = n_left + CORES * n_row
    sources = refs[:n_source]
    out_ref, right_ref, carry_ref, plan = refs[n_source + 1 :][:4]
    acc, fact_buf, code_buf, code_sem, store_sem = refs[n_source + 5 :]
    r = lax.axis_index("row")
    c = lax.axis_index("col")
    z, core = lax.div(c, CORES), lax.rem(c, CORES)
    lefts, rights = sources[:n_left], sources[n_left:]
    rows, width = lefts[0].shape[-1], acc.shape[-1]
    tiles = per_row * per_col
    stations = CORES * n_row * n_chip

    for index in range(CORES * n_row):
        for s in range(n_chip):
            station = index * n_chip + s
            meta = rights[index][s, slots * rows :].astype(jnp.float32)
            for i in range(slots + 1):
                fact_buf[i, station : station + 1, :] = meta[i : i + 1]
    by_tile = acc.shape[0] > tiles
    lines = plan_of(fact_buf, r, z, core, n_row, n_chip, slots, per_col, tiles, by_tile)
    for n, line in enumerate(lines):
        code_buf[n : n + 1, :] = line
    to_smem = pltpu.make_async_copy(code_buf, plan, code_sem)
    to_smem.start()
    kept = 0
    for other in range(CORES):
        for j in range(n_row):
            for s in late[other]:
                right_ref[kept] = rights[other * n_row + j][s, : slots * rows]
                kept += 1
    to_smem.wait()

    def group(other, j):
        index = other * n_row + j

        def station(m, s):
            first = j * slots * width

            def left():
                return lefts[len(early[0]) * other + m][first : first + slots * width]

            def right():
                tiles = [rights[index][s, i * rows : (i + 1) * rows] for i in range(slots)]
                return jnp.concatenate(tiles, axis=1)

            return index * n_chip + s, left, right

        found = [station(m, s) for m, s in enumerate(early[other])]
        return 1, lambda step: found

    groups = [group(other, j) for other in range(CORES) for j in range(n_row)]
    number = settle(plan, groups, stations, slots, acc, None, out_ref, per_col, store_sem)

    def hand_on(place, column):
        before = plan[2, column]
        carry_ref[place] = jnp.where(before < 0, 0.0, acc[jnp.maximum(before, 0)])

    def hand_step(index, carry):
        column = index * n_chip + n_chip // 2
        each_hit(plan, [column + n * stations for n in range(slots * slots)], 1, hand_on)
        return carry

    lax.fori_loop(0, CORES * n_row, hand_step, 0)
    drain(number, acc, store_sem)


def main_part(left, right, out, n_row, per_row, per_col):
    n_chip = len(left[0]) + 1
    early, late = parts_of(n_chip)
    flat = [*left[0], *left[1]]
    rows, width = flat[0].shape[1], right[0].shape[2]
    slots = right[0].shape[1] // rows
    tiles = per_row * per_col
    stations = CORES * n_row * n_chip
    pairs = slots * slots * stations
    places = min(tiles + 1, pairs)
    by_tile = places > tiles
    tail_places = (places if by_tile else slots * slots * CORES * n_row, width, width)
    plan = (8, pairs)
    sources = [*flat, *right]
    anywhere = pl.BlockSpec(memory_space=pl.ANY)
    held = (
        (places + tail_places[0]) * width * width * 4
        + sum(x.size for x in sources) * 2
        + n_row * sum(map(len, late)) * (slots * rows + META) * width * 2
        + (slots + 1) * stations * width * 4
        + 8 * pairs * pairs * 4
    )
    return pl.pallas_call(
        functools.partial(main_kernel, n_row, n_chip, slots, per_row, per_col),
        out_shape=[
            jax.ShapeDtypeStruct(out.shape, out.dtype),
            jax.ShapeDtypeStruct(
                (n_row * sum(map(len, late)), slots * rows, width), jnp.bfloat16
            ),
            jax.ShapeDtypeStruct(tail_places, jnp.float32),
            jax.ShapeDtypeStruct(plan, jnp.int32),
        ],
        in_specs=[pl.BlockSpec(memory_space=pltpu.VMEM)] * len(sources) + [anywhere],
        out_specs=[
            anywhere,
            pl.BlockSpec(memory_space=pltpu.VMEM),
            pl.BlockSpec(memory_space=pltpu.VMEM),
            pl.BlockSpec(memory_space=pltpu.SMEM),
        ],
        scratch_shapes=[
            pltpu.VMEM((places, width, width), jnp.float32),
            pltpu.VMEM((slots + 1, stations, width), jnp.float32),
            pltpu.VMEM(plan, jnp.int32),
            pltpu.SemaphoreType.DMA,
            pltpu.SemaphoreType.DMA,
        ],
        input_output_aliases={len(sources): 0},
        compiler_params=pltpu.CompilerParams(vmem_limit_bytes=held + 3 * MIB),
        cost_estimate=pl.CostEstimate(flops=0, bytes_accessed=0, transcendentals=0),
    )(*sources, out)


def tail_kernel(n_row, n_chip, slots, per_col, plan, *refs):
    _, late = parts_of(n_chip)
    n_left = sum(map(len, late))
    lefts, right_ref, base_ref = refs[:n_left], refs[n_left], refs[n_left + 1]
    out_ref, acc, store_sem = refs[n_left + 3 :]
    rows, width = lefts[0].shape[-1], acc.shape[-1]
    stations = CORES * n_row * n_chip

    found = []
    for other in range(CORES):
        for j in range(n_row):
            for m, s in enumerate(late[other]):
                source = lefts[len(late[0]) * other + m]

                def left(source=source, j=j):
                    return source[j * slots * width : (j + 1) * slots * width]

                def right(kept=len(found)):
                    tiles = [right_ref[kept, i * rows : (i + 1) * rows] for i in range(slots)]
                    return jnp.concatenate(tiles, axis=1)

                found.append(((other * n_row + j) * n_chip + s, left, right))
    groups = [(1, lambda step: found)]
    number = settle(plan, groups, stations, slots, acc, base_ref, out_ref, per_col, store_sem)
    drain(number, acc, store_sem)


def tail_part(left, right, base, plan, out, n_row, per_row, per_col):
    flat = [*left[0], *left[1]]
    _, depth, width = right.shape
    slots = depth // flat[0].shape[1]
    stations = plan.shape[1] // slots**2
    n_chip = stations // (CORES * n_row)
    anywhere = pl.BlockSpec(memory_space=pl.ANY)
    vmem = pl.BlockSpec(memory_space=pltpu.VMEM)
    smem = pl.BlockSpec(memory_space=pltpu.SMEM)
    held = 3 * base.size * 4 + 2 * right.size * 2 + 2 * MIB * len(flat)
    return pl.pallas_call(
        functools.partial(tail_kernel, n_row, n_chip, slots, per_col),
        out_shape=jax.ShapeDtypeStruct(out.shape, out.dtype),
        in_specs=[smem] + [vmem] * (len(flat) + 2) + [anywhere],
        out_specs=anywhere,
        scratch_shapes=[
            pltpu.VMEM(base.shape, jnp.float32),
            pltpu.SemaphoreType.DMA,
        ],
        input_output_aliases={len(flat) + 3: 0},
        compiler_params=pltpu.CompilerParams(vmem_limit_bytes=held + 4 * MIB),
        cost_estimate=pl.CostEstimate(flops=0, bytes_accessed=0, transcendentals=0),
    )(plan, *flat, right, base, out)


def zero_kernel(first, count, *refs):
    out_ref, block, sem = refs[-3:]
    block[...] = jnp.zeros_like(block)
    height = block.shape[0]
    copies = [
        pltpu.make_async_copy(block, out_ref.at[pl.ds((first + n) * height, height)], sem.at[n])
        for n in range(count)
    ]
    for copy in copies:
        copy.start()
    for copy in copies:
        copy.wait()


def zero_part(height, width, part, after, out=None):
    step = 128
    count = height // step
    early = count * ZERO_EARLY // 16
    first, number = ((0, early), (early, count - early))[part]
    anywhere = pl.BlockSpec(memory_space=pl.ANY)
    inputs = [after] if out is None else [after, out]
    return pl.pallas_call(
        functools.partial(zero_kernel, first, number),
        out_shape=jax.ShapeDtypeStruct((height, width), jnp.float32),
        in_specs=[anywhere] * len(inputs),
        out_specs=anywhere,
        scratch_shapes=[
            pltpu.VMEM((step, width), jnp.float32),
            pltpu.SemaphoreType.DMA((number,)),
        ],
        input_output_aliases={} if out is None else {1: 0},
        compiler_params=pltpu.CompilerParams(vmem_limit_bytes=4 * MIB),
        cost_estimate=pl.CostEstimate(
            flops=0, bytes_accessed=height * width * 2, transcendentals=0
        ),
    )(*inputs)


def local(sensitivity, tile_ids, counts, weight_class):
    n_row = lax.axis_size("row")
    n_col = lax.axis_size("col")
    n_chip = n_col // CORES
    width = sensitivity.shape[-1]
    per_row = TILES // n_row
    per_col = TILES // n_col
    middle = n_chip // 2

    def flip_row(value, j):
        return lax.ppermute(value, "row", [(i, i ^ j) for i in range(n_row)])

    def shift_chip(value, s):
        pairs = [(i, (i + CORES * s) % n_col) for i in range(n_col)]
        return lax.ppermute(value, "col", pairs)

    def flip_core(value):
        return lax.ppermute(value, "col", [(i, i ^ 1) for i in range(n_col)])

    def pad(value, extra):
        return jnp.pad(value, ((0, extra), (0, 0)))

    after = lax.optimization_barrier

    ids = jnp.transpose(tile_ids, (0, 2, 1))[0]
    parts = pack(sensitivity[0], weight_class, ids, counts, n_chip)
    to_row, to_chip = parts[:n_row], parts[n_row:]
    plane = [to_row[0]] + [flip_row(to_row[j], j) for j in range(1, n_row)]
    from_chip = [to_chip[0]] + [shift_chip(to_chip[s], s) for s in range(1, n_chip)]
    height, breadth = per_row * width, per_col * width
    zeros = zero_part(height, breadth, 0, to_chip[0])
    plane, from_chip, zeros = after((plane, from_chip, zeros))
    rows = sensitivity.shape[-2]
    chip = jnp.stack(plane).reshape(-1, rows)
    near = {0: chip}
    for s in range(1, middle):
        near[s] = shift_chip(near[s - 1], 1)
        near[n_chip - s] = shift_chip(pad(chip, 32) if s == 1 else near[n_chip - s + 1], -1)
    right = jnp.stack(from_chip)
    own = [flip_core(chip), flip_core(right)]
    *own, again, token = after((*own, right, to_chip[0]))
    sides = [right] + [flip_row(right if j == 1 else again, j) for j in range(1, n_row)]
    far = shift_chip(pad(near[middle - 1], 48), 1)
    swapped = {s: flip_core(near[s]) for s in range(1, middle)}
    zeros = zero_part(height, breadth, 1, token, zeros)
    swapped, waiting, zeros = after((swapped, sides[1:], zeros))
    swapped |= {s: flip_core(near[s]) for s in near if s > middle} | {0: own[0]}
    sides += [own[1]] + [flip_core(x) for x in waiting]
    early = [[near[s] for s in sorted(near)], [swapped[s] for s in sorted(swapped)]]
    out, tail_right, base, plan = main_part(early, sides, zeros, n_row, per_row, per_col)
    far, plan = after((far, plan))
    return tail_part(
        [[far], [flip_core(far)]], tail_right, base, plan, out, n_row, per_row, per_col
    )


def solution(mesh):
    in_specs = (
        P(("row", "col"), None, None, None, None),
        P(("row", "col"), None, None),
        P(("row", "col"), None),
        P(("row", "col"), None),
    )
    return jax.shard_map(
        local, mesh=mesh, in_specs=in_specs, out_specs=P("row", "col"), check_vma=False
    )
```

```python
import functools

import jax
import jax.numpy as jnp
from jax import lax
from jax.experimental import pallas as pl
from jax.experimental.pallas import tpu as pltpu
from jax.sharding import PartitionSpec as P

TILES = 128
CORES = 2
META = 16
TAIL_GROUP = 2
ZERO_EARLY = 6
MIB = 1024 * 1024


def scale_of(class_ref):
    classes = class_ref[...]
    return jnp.where(
        classes == 0, 1.0, jnp.where(classes == 1, 0.5, jnp.where(classes == 2, 0.25, 0.125))
    ).astype(jnp.float32)


def pack_kernel(n_row, n_chip, slots, sens_ref, class_ref, ids_ref, counts_ref, *refs):
    outs, meta_ref = refs[:-1], refs[-1]
    r = lax.axis_index("row")
    z = lax.div(lax.axis_index("col"), CORES)
    rows, width = sens_ref.shape[2:]
    scale = scale_of(class_ref)
    for j in range(n_row):
        for i in range(slots):
            tile = sens_ref[r ^ j, i].T.astype(jnp.float32) * scale
            outs[j][i * width : (i + 1) * width] = tile.astype(jnp.bfloat16)
    scale = jnp.broadcast_to(scale, (width, rows)).T
    meta_ref[...] = jnp.zeros_like(meta_ref)
    meta_ref[:slots, :n_row] = ids_ref[...].astype(jnp.float32)
    meta_ref[slots : slots + 1, :n_row] = counts_ref[...].astype(jnp.float32)
    meta = meta_ref[...].astype(jnp.bfloat16)
    for s in range(n_chip):
        owner = lax.rem(z + s, n_chip)
        out = outs[n_row + s]
        for i in range(slots):
            tile = sens_ref[owner, i].astype(jnp.float32) * scale
            out[i * rows : (i + 1) * rows] = tile.astype(jnp.bfloat16)
        out[slots * rows :] = meta


def pack(sensitivity, weight_class, ids, counts, n_chip):
    n_row, slots, rows, width = sensitivity.shape
    vmem = pl.BlockSpec(memory_space=pltpu.VMEM)
    return pl.pallas_call(
        functools.partial(pack_kernel, n_row, n_chip, slots),
        out_shape=[jax.ShapeDtypeStruct((slots * width, rows), jnp.bfloat16)] * n_row
        + [jax.ShapeDtypeStruct((slots * rows + META, width), jnp.bfloat16)] * n_chip,
        in_specs=[vmem] * 4,
        out_specs=[vmem] * (n_row + n_chip),
        scratch_shapes=[pltpu.VMEM((META, width), jnp.float32)],
        cost_estimate=pl.CostEstimate(flops=0, bytes_accessed=0, transcendentals=0),
    )(sensitivity, weight_class, ids, counts)


def plan_of(facts, r, z, core, n_row, n_chip, slots, per_col, none, by_tile):
    _, stations, width = facts.shape
    lane = lax.broadcasted_iota(jnp.int32, (stations, width), 1)

    def pick(row, owner):
        return jnp.sum(jnp.where(lane == owner, facts[row], 0.0), axis=1, keepdims=True)

    used_left, used_right = pick(slots, r), pick(slots, z)
    lefts = [pick(i, r) for i in range(slots)]
    rights = [pick(j, z) - (core * per_col).astype(jnp.float32) for j in range(slots)]
    column = []
    for i in range(slots):
        for j in range(slots):
            met = (i < used_left) & (j < used_right) & (rights[j] >= 0) & (rights[j] < per_col)
            column.append(jnp.where(met, lefts[i] * per_col + rights[j], float(none)))
    count = len(column) * stations
    tile = jnp.broadcast_to(jnp.concatenate(column, axis=0), (count, count))
    other = tile.T

    def part_of(axis):
        pair = lax.broadcasted_iota(jnp.int32, (count, count), axis)
        station = lax.rem(pair, stations)
        s = lax.rem(station, n_chip)
        tail = s == n_chip // 2
        number = jnp.where(tail, lax.div(station, n_chip), station) * len(column)
        return tail, (number + lax.div(pair, stations)).astype(jnp.float32)

    tail_down, number_down = part_of(0)
    tail_across, number_across = part_of(1)
    same = (tile == other) & (tail_down == tail_across)
    first = jnp.min(jnp.where(same, number_down, 1e6), axis=0, keepdims=True)
    fresh = (first == number_across[:1]).astype(jnp.float32)
    last = jnp.max(jnp.where(same, number_down, -1.0), axis=0, keepdims=True)
    final = (last == number_across[:1]).astype(jnp.float32)
    real = (other[:1] < none).astype(jnp.float32)
    place = other[:1] if by_tile else first
    met = (tile == other) & jnp.logical_not(tail_down)
    met = jnp.min(jnp.where(met, number_down, 1e6), axis=0, keepdims=True)
    before = jnp.where(met < 1e6, other[:1] if by_tile else met, -1.0)
    code = 8.0 * place + 4.0 * final * real + 2.0 * fresh * real + fresh
    return [row.astype(jnp.int32) for row in (code, other[:1], before)]


def each_hit(plan, columns, flag, act):
    number = 0
    for column in columns:
        code = plan[0, column]
        hit = lax.shift_right_logical(code, flag) & 1

        @pl.when(hit == 1)
        def _():
            act(lax.shift_right_logical(code, 3), column)

        number = number + hit
    return number


def settle(plan, groups, stations, slots, acc, base, out_ref, per_col, store_sem):
    width = acc.shape[-1]
    pairs = slots * slots

    def store(place, column):
        block = block_of(out_ref, plan[1, column], per_col, width)
        pltpu.make_async_copy(acc.at[place], block, store_sem).start()

    def add(column, left, right):
        gram = jnp.dot(left(), right(), preferred_element_type=jnp.float32)
        for n in range(pairs):
            code = plan[0, column + n * stations]
            place, fresh = lax.shift_right_logical(code, 3), code & 1
            i, j = divmod(n, slots)
            part = gram[i * width : (i + 1) * width, j * width : (j + 1) * width]
            start = part if base is None else base[place] + part
            acc[place] = jnp.where(fresh == 1, start, acc[place] + part)

    def add_store(found):
        for column, left, right in found:
            add(column, left, right)
        columns = [column + n * stations for column, _, _ in found for n in range(pairs)]
        return each_hit(plan, columns, 2, store)

    total = 0
    for steps, stations_of in groups:
        if steps == 1:
            total = total + add_store(stations_of(0))
        else:
            total = lax.fori_loop(
                0, steps, lambda step, sofar: sofar + add_store(stations_of(step)), total
            )
    return total


def drain(number, acc, sem):
    def step(index, carry):
        pltpu.make_async_copy(acc.at[0], acc.at[0], sem).wait()
        return carry

    lax.fori_loop(0, number, step, 0)


def parts_of(n_chip):
    far = n_chip // 2
    near = [s for s in range(n_chip) if s != far]
    return [near] * CORES, [[far]] * CORES


def block_of(out_ref, tile, per_col, width):
    rows = pl.ds(pl.multiple_of(lax.div(tile, per_col) * width, width), width)
    columns = pl.ds(pl.multiple_of(lax.rem(tile, per_col) * width, width), width)
    return out_ref.at[rows, columns]


def main_kernel(n_row, n_chip, slots, per_row, per_col, *refs):
    early, late = parts_of(n_chip)
    n_left = sum(map(len, early))
    n_source = n_left + CORES * n_row
    sources = refs[:n_source]
    out_ref, right_ref, carry_ref, plan = refs[n_source + 1 :][:4]
    acc, fact_buf, code_buf, code_sem, store_sem = refs[n_source + 5 :]
    r = lax.axis_index("row")
    c = lax.axis_index("col")
    z, core = lax.div(c, CORES), lax.rem(c, CORES)
    lefts, rights = sources[:n_left], sources[n_left:]
    rows, width = lefts[0].shape[-1], acc.shape[-1]
    tiles = per_row * per_col
    stations = CORES * n_row * n_chip

    for index in range(CORES * n_row):
        for s in range(n_chip):
            station = index * n_chip + s
            meta = rights[index][s, slots * rows :].astype(jnp.float32)
            for i in range(slots + 1):
                fact_buf[i, station : station + 1, :] = meta[i : i + 1]
    by_tile = acc.shape[0] > tiles
    lines = plan_of(fact_buf, r, z, core, n_row, n_chip, slots, per_col, tiles, by_tile)
    for n, line in enumerate(lines):
        code_buf[n : n + 1, :] = line
    to_smem = pltpu.make_async_copy(code_buf, plan, code_sem)
    to_smem.start()
    kept = 0
    for other in range(CORES):
        for j in range(n_row):
            for s in late[other]:
                right_ref[kept] = rights[other * n_row + j][s, : slots * rows]
                kept += 1
    to_smem.wait()

    def group(other, j):
        index = other * n_row + j

        def station(m, s):
            first = j * slots * width

            def left():
                return lefts[len(early[0]) * other + m][first : first + slots * width]

            def right():
                tiles = [rights[index][s, i * rows : (i + 1) * rows] for i in range(slots)]
                return jnp.concatenate(tiles, axis=1)

            return index * n_chip + s, left, right

        found = [station(m, s) for m, s in enumerate(early[other])]
        return 1, lambda step: found

    groups = [group(other, j) for other in range(CORES) for j in range(n_row)]
    number = settle(plan, groups, stations, slots, acc, None, out_ref, per_col, store_sem)

    def hand_on(place, column):
        before = plan[2, column]
        carry_ref[place] = jnp.where(before < 0, 0.0, acc[jnp.maximum(before, 0)])

    def hand_step(index, carry):
        column = index * n_chip + n_chip // 2
        each_hit(plan, [column + n * stations for n in range(slots * slots)], 1, hand_on)
        return carry

    lax.fori_loop(0, CORES * n_row, hand_step, 0)
    drain(number, acc, store_sem)


def main_part(left, right, out, n_row, per_row, per_col):
    n_chip = len(left[0]) + 1
    early, late = parts_of(n_chip)
    flat = [*left[0], *left[1]]
    rows, width = flat[0].shape[1], right[0].shape[2]
    slots = right[0].shape[1] // rows
    tiles = per_row * per_col
    stations = CORES * n_row * n_chip
    pairs = slots * slots * stations
    places = min(tiles + 1, pairs)
    by_tile = places > tiles
    tail_places = (places if by_tile else slots * slots * CORES * n_row, width, width)
    plan = (8, pairs)
    sources = [*flat, *right]
    anywhere = pl.BlockSpec(memory_space=pl.ANY)
    held = (
        (places + tail_places[0]) * width * width * 4
        + sum(x.size for x in sources) * 2
        + n_row * sum(map(len, late)) * (slots * rows + META) * width * 2
        + (slots + 1) * stations * width * 4
        + 8 * pairs * pairs * 4
    )
    return pl.pallas_call(
        functools.partial(main_kernel, n_row, n_chip, slots, per_row, per_col),
        out_shape=[
            jax.ShapeDtypeStruct(out.shape, out.dtype),
            jax.ShapeDtypeStruct(
                (n_row * sum(map(len, late)), slots * rows, width), jnp.bfloat16
            ),
            jax.ShapeDtypeStruct(tail_places, jnp.float32),
            jax.ShapeDtypeStruct(plan, jnp.int32),
        ],
        in_specs=[pl.BlockSpec(memory_space=pltpu.VMEM)] * len(sources) + [anywhere],
        out_specs=[
            anywhere,
            pl.BlockSpec(memory_space=pltpu.VMEM),
            pl.BlockSpec(memory_space=pltpu.VMEM),
            pl.BlockSpec(memory_space=pltpu.SMEM),
        ],
        scratch_shapes=[
            pltpu.VMEM((places, width, width), jnp.float32),
            pltpu.VMEM((slots + 1, stations, width), jnp.float32),
            pltpu.VMEM(plan, jnp.int32),
            pltpu.SemaphoreType.DMA,
            pltpu.SemaphoreType.DMA,
        ],
        input_output_aliases={len(sources): 0},
        compiler_params=pltpu.CompilerParams(vmem_limit_bytes=held + 3 * MIB),
        cost_estimate=pl.CostEstimate(flops=0, bytes_accessed=0, transcendentals=0),
    )(*sources, out)


def tail_kernel(n_row, n_chip, slots, per_col, plan, *refs):
    _, late = parts_of(n_chip)
    n_left = sum(map(len, late))
    lefts, right_ref, base_ref = refs[:n_left], refs[n_left], refs[n_left + 1]
    out_ref, acc, store_sem = refs[n_left + 3 :]
    rows, width = lefts[0].shape[-1], acc.shape[-1]
    stations = CORES * n_row * n_chip

    found = []
    for other in range(CORES):
        for j in range(n_row):
            for m, s in enumerate(late[other]):
                source = lefts[len(late[0]) * other + m]

                def left(source=source, j=j):
                    return source[j * slots * width : (j + 1) * slots * width]

                def right(kept=len(found)):
                    tiles = [right_ref[kept, i * rows : (i + 1) * rows] for i in range(slots)]
                    return jnp.concatenate(tiles, axis=1)

                found.append(((other * n_row + j) * n_chip + s, left, right))
    groups = [
        (1, lambda step, first=first: found[first : first + TAIL_GROUP])
        for first in range(0, len(found), TAIL_GROUP)
    ]
    number = settle(plan, groups, stations, slots, acc, base_ref, out_ref, per_col, store_sem)
    drain(number, acc, store_sem)


def tail_part(left, right, base, plan, out, n_row, per_row, per_col):
    flat = [*left[0], *left[1]]
    _, depth, width = right.shape
    slots = depth // flat[0].shape[1]
    stations = plan.shape[1] // slots**2
    n_chip = stations // (CORES * n_row)
    anywhere = pl.BlockSpec(memory_space=pl.ANY)
    vmem = pl.BlockSpec(memory_space=pltpu.VMEM)
    smem = pl.BlockSpec(memory_space=pltpu.SMEM)
    held = 3 * base.size * 4 + 2 * right.size * 2 + 2 * MIB * len(flat)
    return pl.pallas_call(
        functools.partial(tail_kernel, n_row, n_chip, slots, per_col),
        out_shape=jax.ShapeDtypeStruct(out.shape, out.dtype),
        in_specs=[smem] + [vmem] * (len(flat) + 2) + [anywhere],
        out_specs=anywhere,
        scratch_shapes=[
            pltpu.VMEM(base.shape, jnp.float32),
            pltpu.SemaphoreType.DMA,
        ],
        input_output_aliases={len(flat) + 3: 0},
        compiler_params=pltpu.CompilerParams(vmem_limit_bytes=held + 4 * MIB),
        cost_estimate=pl.CostEstimate(flops=0, bytes_accessed=0, transcendentals=0),
    )(plan, *flat, right, base, out)


def zero_kernel(first, count, *refs):
    out_ref, block, sem = refs[-3:]
    block[...] = jnp.zeros_like(block)
    height = block.shape[0]
    copies = [
        pltpu.make_async_copy(block, out_ref.at[pl.ds((first + n) * height, height)], sem.at[n])
        for n in range(count)
    ]
    for copy in copies:
        copy.start()
    for copy in copies:
        copy.wait()


def zero_part(height, width, part, after, out=None):
    step = 128
    count = height // step
    early = count * ZERO_EARLY // 16
    first, number = ((0, early), (early, count - early))[part]
    anywhere = pl.BlockSpec(memory_space=pl.ANY)
    inputs = [after] if out is None else [after, out]
    return pl.pallas_call(
        functools.partial(zero_kernel, first, number),
        out_shape=jax.ShapeDtypeStruct((height, width), jnp.float32),
        in_specs=[anywhere] * len(inputs),
        out_specs=anywhere,
        scratch_shapes=[
            pltpu.VMEM((step, width), jnp.float32),
            pltpu.SemaphoreType.DMA((number,)),
        ],
        input_output_aliases={} if out is None else {1: 0},
        compiler_params=pltpu.CompilerParams(vmem_limit_bytes=4 * MIB),
        cost_estimate=pl.CostEstimate(
            flops=0, bytes_accessed=height * width * 2, transcendentals=0
        ),
    )(*inputs)


def local(sensitivity, tile_ids, counts, weight_class):
    n_row = lax.axis_size("row")
    n_col = lax.axis_size("col")
    n_chip = n_col // CORES
    width = sensitivity.shape[-1]
    per_row = TILES // n_row
    per_col = TILES // n_col
    middle = n_chip // 2

    def flip_row(value, j):
        return lax.ppermute(value, "row", [(i, i ^ j) for i in range(n_row)])

    def shift_chip(value, s):
        pairs = [(i, (i + CORES * s) % n_col) for i in range(n_col)]
        return lax.ppermute(value, "col", pairs)

    def flip_core(value):
        return lax.ppermute(value, "col", [(i, i ^ 1) for i in range(n_col)])

    def pad(value, extra):
        return jnp.pad(value, ((0, extra), (0, 0)))

    after = lax.optimization_barrier

    ids = jnp.transpose(tile_ids, (0, 2, 1))[0]
    parts = pack(sensitivity[0], weight_class, ids, counts, n_chip)
    to_row, to_chip = parts[:n_row], parts[n_row:]
    plane = [to_row[0]] + [flip_row(to_row[j], j) for j in range(1, n_row)]
    from_chip = [to_chip[0]] + [shift_chip(to_chip[s], s) for s in range(1, n_chip)]
    height, breadth = per_row * width, per_col * width
    zeros = zero_part(height, breadth, 0, to_chip[0])
    plane, from_chip, zeros = after((plane, from_chip, zeros))
    rows = sensitivity.shape[-2]
    chip = jnp.stack(plane).reshape(-1, rows)
    near = {0: chip}
    for s in range(1, middle):
        near[s] = shift_chip(near[s - 1], 1)
        near[n_chip - s] = shift_chip(pad(chip, 32) if s == 1 else near[n_chip - s + 1], -1)
    right = jnp.stack(from_chip)
    own = [flip_core(chip), flip_core(right)]
    *own, again, token = after((*own, right, to_chip[0]))
    sides = [right] + [flip_row(right if j == 1 else again, j) for j in range(1, n_row)]
    far = shift_chip(pad(near[middle - 1], 48), 1)
    swapped = {s: flip_core(near[s]) for s in range(1, middle)}
    zeros = zero_part(height, breadth, 1, token, zeros)
    swapped, waiting, zeros = after((swapped, sides[1:], zeros))
    swapped |= {s: flip_core(near[s]) for s in near if s > middle} | {0: own[0]}
    sides += [own[1]] + [flip_core(x) for x in waiting]
    early = [[near[s] for s in sorted(near)], [swapped[s] for s in sorted(swapped)]]
    out, tail_right, base, plan = main_part(early, sides, zeros, n_row, per_row, per_col)
    far, plan = after((far, plan))
    return tail_part(
        [[far], [flip_core(far)]], tail_right, base, plan, out, n_row, per_row, per_col
    )


def solution(mesh):
    in_specs = (
        P(("row", "col"), None, None, None, None),
        P(("row", "col"), None, None),
        P(("row", "col"), None),
        P(("row", "col"), None),
    )
    return jax.shard_map(
        local, mesh=mesh, in_specs=in_specs, out_specs=P("row", "col"), check_vma=False
    )
```

```python
import functools

import jax
import jax.numpy as jnp
from jax import lax
from jax.experimental import pallas as pl
from jax.experimental.pallas import tpu as pltpu
from jax.sharding import PartitionSpec as P

TILES = 128
CORES = 2
META = 16
TAIL_GROUP = 1
ZERO_EARLY = 6
MIB = 1024 * 1024


def scale_of(class_ref):
    classes = class_ref[...]
    return jnp.where(
        classes == 0, 1.0, jnp.where(classes == 1, 0.5, jnp.where(classes == 2, 0.25, 0.125))
    ).astype(jnp.float32)


def pack_kernel(n_row, n_chip, slots, sens_ref, class_ref, ids_ref, counts_ref, *refs):
    outs, meta_ref = refs[:-1], refs[-1]
    r = lax.axis_index("row")
    z = lax.div(lax.axis_index("col"), CORES)
    rows, width = sens_ref.shape[2:]
    scale = scale_of(class_ref)
    for j in range(n_row):
        for i in range(slots):
            tile = sens_ref[r ^ j, i].T.astype(jnp.float32) * scale
            outs[j][i * width : (i + 1) * width] = tile.astype(jnp.bfloat16)
    scale = jnp.broadcast_to(scale, (width, rows)).T
    meta_ref[...] = jnp.zeros_like(meta_ref)
    meta_ref[:slots, :n_row] = ids_ref[...].astype(jnp.float32)
    meta_ref[slots : slots + 1, :n_row] = counts_ref[...].astype(jnp.float32)
    meta = meta_ref[...].astype(jnp.bfloat16)
    for s in range(n_chip):
        owner = lax.rem(z + s, n_chip)
        out = outs[n_row + s]
        for i in range(slots):
            tile = sens_ref[owner, i].astype(jnp.float32) * scale
            out[i * rows : (i + 1) * rows] = tile.astype(jnp.bfloat16)
        out[slots * rows :] = meta


def pack(sensitivity, weight_class, ids, counts, n_chip):
    n_row, slots, rows, width = sensitivity.shape
    vmem = pl.BlockSpec(memory_space=pltpu.VMEM)
    return pl.pallas_call(
        functools.partial(pack_kernel, n_row, n_chip, slots),
        out_shape=[jax.ShapeDtypeStruct((slots * width, rows), jnp.bfloat16)] * n_row
        + [jax.ShapeDtypeStruct((slots * rows + META, width), jnp.bfloat16)] * n_chip,
        in_specs=[vmem] * 4,
        out_specs=[vmem] * (n_row + n_chip),
        scratch_shapes=[pltpu.VMEM((META, width), jnp.float32)],
        cost_estimate=pl.CostEstimate(flops=0, bytes_accessed=0, transcendentals=0),
    )(sensitivity, weight_class, ids, counts)


def plan_of(facts, r, z, core, n_row, n_chip, slots, per_col, none, by_tile):
    _, stations, width = facts.shape
    lane = lax.broadcasted_iota(jnp.int32, (stations, width), 1)

    def pick(row, owner):
        return jnp.sum(jnp.where(lane == owner, facts[row], 0.0), axis=1, keepdims=True)

    used_left, used_right = pick(slots, r), pick(slots, z)
    lefts = [pick(i, r) for i in range(slots)]
    rights = [pick(j, z) - (core * per_col).astype(jnp.float32) for j in range(slots)]
    column = []
    for i in range(slots):
        for j in range(slots):
            met = (i < used_left) & (j < used_right) & (rights[j] >= 0) & (rights[j] < per_col)
            column.append(jnp.where(met, lefts[i] * per_col + rights[j], float(none)))
    count = len(column) * stations
    tile = jnp.broadcast_to(jnp.concatenate(column, axis=0), (count, count))
    other = tile.T

    def part_of(axis):
        pair = lax.broadcasted_iota(jnp.int32, (count, count), axis)
        station = lax.rem(pair, stations)
        s = lax.rem(station, n_chip)
        tail = s == n_chip // 2
        number = jnp.where(tail, lax.div(station, n_chip), station) * len(column)
        return tail, (number + lax.div(pair, stations)).astype(jnp.float32)

    tail_down, number_down = part_of(0)
    tail_across, number_across = part_of(1)
    same = (tile == other) & (tail_down == tail_across)
    first = jnp.min(jnp.where(same, number_down, 1e6), axis=0, keepdims=True)
    fresh = (first == number_across[:1]).astype(jnp.float32)
    last = jnp.max(jnp.where(same, number_down, -1.0), axis=0, keepdims=True)
    final = (last == number_across[:1]).astype(jnp.float32)
    real = (other[:1] < none).astype(jnp.float32)
    place = other[:1] if by_tile else first
    met = (tile == other) & jnp.logical_not(tail_down)
    met = jnp.min(jnp.where(met, number_down, 1e6), axis=0, keepdims=True)
    before = jnp.where(met < 1e6, other[:1] if by_tile else met, -1.0)
    code = 8.0 * place + 4.0 * final * real + 2.0 * fresh * real + fresh
    return [row.astype(jnp.int32) for row in (code, other[:1], before)]


def each_hit(plan, columns, flag, act):
    number = 0
    for column in columns:
        code = plan[0, column]
        hit = lax.shift_right_logical(code, flag) & 1

        @pl.when(hit == 1)
        def _():
            act(lax.shift_right_logical(code, 3), column)

        number = number + hit
    return number


def settle(plan, groups, stations, slots, acc, base, out_ref, per_col, store_sem):
    width = acc.shape[-1]
    pairs = slots * slots

    def store(place, column):
        block = block_of(out_ref, plan[1, column], per_col, width)
        pltpu.make_async_copy(acc.at[place], block, store_sem).start()

    def add(column, left, right):
        gram = jnp.dot(left(), right(), preferred_element_type=jnp.float32)
        for n in range(pairs):
            code = plan[0, column + n * stations]
            place, fresh = lax.shift_right_logical(code, 3), code & 1
            i, j = divmod(n, slots)
            part = gram[i * width : (i + 1) * width, j * width : (j + 1) * width]
            start = part if base is None else base[place] + part
            acc[place] = jnp.where(fresh == 1, start, acc[place] + part)

    def add_store(found):
        for column, left, right in found:
            add(column, left, right)
        columns = [column + n * stations for column, _, _ in found for n in range(pairs)]
        return each_hit(plan, columns, 2, store)

    total = 0
    for steps, stations_of in groups:
        if steps == 1:
            total = total + add_store(stations_of(0))
        else:
            total = lax.fori_loop(
                0, steps, lambda step, sofar: sofar + add_store(stations_of(step)), total
            )
    return total


def drain(number, acc, sem):
    def step(index, carry):
        pltpu.make_async_copy(acc.at[0], acc.at[0], sem).wait()
        return carry

    lax.fori_loop(0, number, step, 0)


def parts_of(n_chip):
    far = n_chip // 2
    near = [s for s in range(n_chip) if s != far]
    return [near] * CORES, [[far]] * CORES


def block_of(out_ref, tile, per_col, width):
    rows = pl.ds(pl.multiple_of(lax.div(tile, per_col) * width, width), width)
    columns = pl.ds(pl.multiple_of(lax.rem(tile, per_col) * width, width), width)
    return out_ref.at[rows, columns]


def main_kernel(n_row, n_chip, slots, per_row, per_col, *refs):
    early, late = parts_of(n_chip)
    n_left = sum(map(len, early))
    n_source = n_left + CORES * n_row
    sources = refs[:n_source]
    out_ref, right_ref, carry_ref, plan = refs[n_source + 1 :][:4]
    acc, fact_buf, code_buf, code_sem, store_sem = refs[n_source + 5 :]
    r = lax.axis_index("row")
    c = lax.axis_index("col")
    z, core = lax.div(c, CORES), lax.rem(c, CORES)
    lefts, rights = sources[:n_left], sources[n_left:]
    rows, width = lefts[0].shape[-1], acc.shape[-1]
    tiles = per_row * per_col
    stations = CORES * n_row * n_chip

    for index in range(CORES * n_row):
        for s in range(n_chip):
            station = index * n_chip + s
            meta = rights[index][s, slots * rows :].astype(jnp.float32)
            for i in range(slots + 1):
                fact_buf[i, station : station + 1, :] = meta[i : i + 1]
    by_tile = acc.shape[0] > tiles
    lines = plan_of(fact_buf, r, z, core, n_row, n_chip, slots, per_col, tiles, by_tile)
    for n, line in enumerate(lines):
        code_buf[n : n + 1, :] = line
    to_smem = pltpu.make_async_copy(code_buf, plan, code_sem)
    to_smem.start()
    kept = 0
    for other in range(CORES):
        for j in range(n_row):
            for s in late[other]:
                right_ref[kept] = rights[other * n_row + j][s, : slots * rows]
                kept += 1
    to_smem.wait()

    def group(other, j):
        index = other * n_row + j

        def station(m, s):
            first = j * slots * width

            def left():
                return lefts[len(early[0]) * other + m][first : first + slots * width]

            def right():
                tiles = [rights[index][s, i * rows : (i + 1) * rows] for i in range(slots)]
                return jnp.concatenate(tiles, axis=1)

            return index * n_chip + s, left, right

        found = [station(m, s) for m, s in enumerate(early[other])]
        return 1, lambda step: found

    groups = [group(other, j) for other in range(CORES) for j in range(n_row)]
    number = settle(plan, groups, stations, slots, acc, None, out_ref, per_col, store_sem)

    def hand_on(place, column):
        before = plan[2, column]
        carry_ref[place] = jnp.where(before < 0, 0.0, acc[jnp.maximum(before, 0)])

    def hand_step(index, carry):
        column = index * n_chip + n_chip // 2
        each_hit(plan, [column + n * stations for n in range(slots * slots)], 1, hand_on)
        return carry

    lax.fori_loop(0, CORES * n_row, hand_step, 0)
    drain(number, acc, store_sem)


def main_part(left, right, out, n_row, per_row, per_col):
    n_chip = len(left[0]) + 1
    early, late = parts_of(n_chip)
    flat = [*left[0], *left[1]]
    rows, width = flat[0].shape[1], right[0].shape[2]
    slots = right[0].shape[1] // rows
    tiles = per_row * per_col
    stations = CORES * n_row * n_chip
    pairs = slots * slots * stations
    places = min(tiles + 1, pairs)
    by_tile = places > tiles
    tail_places = (places if by_tile else slots * slots * CORES * n_row, width, width)
    plan = (8, pairs)
    sources = [*flat, *right]
    anywhere = pl.BlockSpec(memory_space=pl.ANY)
    held = (
        (places + tail_places[0]) * width * width * 4
        + sum(x.size for x in sources) * 2
        + n_row * sum(map(len, late)) * (slots * rows + META) * width * 2
        + (slots + 1) * stations * width * 4
        + 8 * pairs * pairs * 4
    )
    return pl.pallas_call(
        functools.partial(main_kernel, n_row, n_chip, slots, per_row, per_col),
        out_shape=[
            jax.ShapeDtypeStruct(out.shape, out.dtype),
            jax.ShapeDtypeStruct(
                (n_row * sum(map(len, late)), slots * rows, width), jnp.bfloat16
            ),
            jax.ShapeDtypeStruct(tail_places, jnp.float32),
            jax.ShapeDtypeStruct(plan, jnp.int32),
        ],
        in_specs=[pl.BlockSpec(memory_space=pltpu.VMEM)] * len(sources) + [anywhere],
        out_specs=[
            anywhere,
            pl.BlockSpec(memory_space=pltpu.VMEM),
            pl.BlockSpec(memory_space=pltpu.VMEM),
            pl.BlockSpec(memory_space=pltpu.SMEM),
        ],
        scratch_shapes=[
            pltpu.VMEM((places, width, width), jnp.float32),
            pltpu.VMEM((slots + 1, stations, width), jnp.float32),
            pltpu.VMEM(plan, jnp.int32),
            pltpu.SemaphoreType.DMA,
            pltpu.SemaphoreType.DMA,
        ],
        input_output_aliases={len(sources): 0},
        compiler_params=pltpu.CompilerParams(vmem_limit_bytes=held + 3 * MIB),
        cost_estimate=pl.CostEstimate(flops=0, bytes_accessed=0, transcendentals=0),
    )(*sources, out)


def tail_kernel(n_row, n_chip, slots, per_col, plan, *refs):
    _, late = parts_of(n_chip)
    n_left = sum(map(len, late))
    lefts, right_ref, base_ref = refs[:n_left], refs[n_left], refs[n_left + 1]
    out_ref, acc, store_sem = refs[n_left + 3 :]
    rows, width = lefts[0].shape[-1], acc.shape[-1]
    stations = CORES * n_row * n_chip

    found = []
    for other in range(CORES):
        for j in range(n_row):
            for m, s in enumerate(late[other]):
                source = lefts[len(late[0]) * other + m]

                def left(source=source, j=j):
                    return source[j * slots * width : (j + 1) * slots * width]

                def right(kept=len(found)):
                    tiles = [right_ref[kept, i * rows : (i + 1) * rows] for i in range(slots)]
                    return jnp.concatenate(tiles, axis=1)

                found.append(((other * n_row + j) * n_chip + s, left, right))
    groups = [
        (1, lambda step, first=first: found[first : first + TAIL_GROUP])
        for first in range(0, len(found), TAIL_GROUP)
    ]
    number = settle(plan, groups, stations, slots, acc, base_ref, out_ref, per_col, store_sem)
    drain(number, acc, store_sem)


def tail_part(left, right, base, plan, out, n_row, per_row, per_col):
    flat = [*left[0], *left[1]]
    _, depth, width = right.shape
    slots = depth // flat[0].shape[1]
    stations = plan.shape[1] // slots**2
    n_chip = stations // (CORES * n_row)
    anywhere = pl.BlockSpec(memory_space=pl.ANY)
    vmem = pl.BlockSpec(memory_space=pltpu.VMEM)
    smem = pl.BlockSpec(memory_space=pltpu.SMEM)
    held = 3 * base.size * 4 + 2 * right.size * 2 + 2 * MIB * len(flat)
    return pl.pallas_call(
        functools.partial(tail_kernel, n_row, n_chip, slots, per_col),
        out_shape=jax.ShapeDtypeStruct(out.shape, out.dtype),
        in_specs=[smem] + [vmem] * (len(flat) + 2) + [anywhere],
        out_specs=anywhere,
        scratch_shapes=[
            pltpu.VMEM(base.shape, jnp.float32),
            pltpu.SemaphoreType.DMA,
        ],
        input_output_aliases={len(flat) + 3: 0},
        compiler_params=pltpu.CompilerParams(vmem_limit_bytes=held + 4 * MIB),
        cost_estimate=pl.CostEstimate(flops=0, bytes_accessed=0, transcendentals=0),
    )(plan, *flat, right, base, out)


def zero_kernel(first, count, *refs):
    out_ref, block, sem = refs[-3:]
    block[...] = jnp.zeros_like(block)
    height = block.shape[0]
    copies = [
        pltpu.make_async_copy(block, out_ref.at[pl.ds((first + n) * height, height)], sem.at[n])
        for n in range(count)
    ]
    for copy in copies:
        copy.start()
    for copy in copies:
        copy.wait()


def zero_part(height, width, part, after, out=None):
    step = 128
    count = height // step
    early = count * ZERO_EARLY // 16
    first, number = ((0, early), (early, count - early))[part]
    anywhere = pl.BlockSpec(memory_space=pl.ANY)
    inputs = [after] if out is None else [after, out]
    return pl.pallas_call(
        functools.partial(zero_kernel, first, number),
        out_shape=jax.ShapeDtypeStruct((height, width), jnp.float32),
        in_specs=[anywhere] * len(inputs),
        out_specs=anywhere,
        scratch_shapes=[
            pltpu.VMEM((step, width), jnp.float32),
            pltpu.SemaphoreType.DMA((number,)),
        ],
        input_output_aliases={} if out is None else {1: 0},
        compiler_params=pltpu.CompilerParams(vmem_limit_bytes=4 * MIB),
        cost_estimate=pl.CostEstimate(
            flops=0, bytes_accessed=height * width * 2, transcendentals=0
        ),
    )(*inputs)


def local(sensitivity, tile_ids, counts, weight_class):
    n_row = lax.axis_size("row")
    n_col = lax.axis_size("col")
    n_chip = n_col // CORES
    width = sensitivity.shape[-1]
    per_row = TILES // n_row
    per_col = TILES // n_col
    middle = n_chip // 2

    def flip_row(value, j):
        return lax.ppermute(value, "row", [(i, i ^ j) for i in range(n_row)])

    def shift_chip(value, s):
        pairs = [(i, (i + CORES * s) % n_col) for i in range(n_col)]
        return lax.ppermute(value, "col", pairs)

    def flip_core(value):
        return lax.ppermute(value, "col", [(i, i ^ 1) for i in range(n_col)])

    def pad(value, extra):
        return jnp.pad(value, ((0, extra), (0, 0)))

    after = lax.optimization_barrier

    ids = jnp.transpose(tile_ids, (0, 2, 1))[0]
    parts = pack(sensitivity[0], weight_class, ids, counts, n_chip)
    to_row, to_chip = parts[:n_row], parts[n_row:]
    plane = [to_row[0]] + [flip_row(to_row[j], j) for j in range(1, n_row)]
    from_chip = [to_chip[0]] + [shift_chip(to_chip[s], s) for s in range(1, n_chip)]
    height, breadth = per_row * width, per_col * width
    zeros = zero_part(height, breadth, 0, to_chip[0])
    plane, from_chip, zeros = after((plane, from_chip, zeros))
    rows = sensitivity.shape[-2]
    chip = jnp.stack(plane).reshape(-1, rows)
    near = {0: chip}
    for s in range(1, middle):
        near[s] = shift_chip(near[s - 1], 1)
        near[n_chip - s] = shift_chip(pad(chip, 32) if s == 1 else near[n_chip - s + 1], -1)
    right = jnp.stack(from_chip)
    own = [flip_core(chip), flip_core(right)]
    *own, again, token = after((*own, right, to_chip[0]))
    sides = [right] + [flip_row(right if j == 1 else again, j) for j in range(1, n_row)]
    far = shift_chip(pad(near[middle - 1], 40), 1)
    swapped = {s: flip_core(near[s]) for s in range(1, middle)}
    zeros = zero_part(height, breadth, 1, token, zeros)
    swapped, waiting, zeros = after((swapped, sides[1:], zeros))
    swapped |= {s: flip_core(near[s]) for s in near if s > middle} | {0: own[0]}
    sides += [own[1]] + [flip_core(x) for x in waiting]
    early = [[near[s] for s in sorted(near)], [swapped[s] for s in sorted(swapped)]]
    out, tail_right, base, plan = main_part(early, sides, zeros, n_row, per_row, per_col)
    far, plan = after((far, plan))
    return tail_part(
        [[far], [flip_core(far)]], tail_right, base, plan, out, n_row, per_row, per_col
    )


def solution(mesh):
    in_specs = (
        P(("row", "col"), None, None, None, None),
        P(("row", "col"), None, None),
        P(("row", "col"), None),
        P(("row", "col"), None),
    )
    return jax.shard_map(
        local, mesh=mesh, in_specs=in_specs, out_specs=P("row", "col"), check_vma=False
    )
```
